256 devices in a mesh: sensor: 8 (over y, core), space: 32 (over z, x).
Axes of the slice: x: 4, y: 4, z: 8, core: 2. Of those that a mesh axis runs over, the one named last changes fastest.
Arguments:
- jacobian: float32 [512, 131072], P('space', 'sensor'), as said below
- residual: float32 [131072], P('sensor'), may hold values from -6 to 6
- damping: float32 [1], replicated, may hold values from 0.3 to 3
Outputs:
- update: float32 [512], replicated
The draws below stay inside these ranges and needn't reach their ends.
Inputs may be any that keep to these rules, and one draw needn't show every extreme that they name: `jacobian`: every column block of the Jacobian has full rank over any 512 observations, which number at least the parameters; the entries are real-valued with row and column scales that vary.
All inputs are finite; a program needn't handle non-finite values.
Results may differ from the reference program's by a relative error of at most 0.00011.
Values sent between devices are 32-bit elements; how exact they have to be, the bound alone decides.
A program may use at most 64 MiB of HBM per device.

```python
import math
import jax
import jax.numpy as jnp
from jax import lax

P_SIZE = 512
M = 131072


def draw_jacobian(key, part):
    first_key, second_key, third_key = jax.random.split(jax.random.fold_in(key, 17), 3)
    row_scale = jnp.exp(jax.random.uniform(first_key, (1, M), jnp.float32) * jnp.log(10.0))
    col_scale = 0.1 * jnp.exp(jax.random.uniform(second_key, (P_SIZE, 1), jnp.float32) * jnp.log(10.0))
    base = jax.random.normal(third_key, (P_SIZE, M), jnp.float32)
    return (base * row_scale * col_scale / (4.0 * jnp.sqrt(float(M)))).astype(jnp.float32)


def level_of(own_key, dims, cuts, least, high):
    gain, own = 1.0, jax.random.fold_in(own_key, 6)
    for dim, parts in cuts:
        heights = jnp.exp(jax.random.uniform(jax.random.fold_in(own, dim), (parts,), jnp.float32, least / len(cuts), high / len(cuts)))
        gain = gain * jnp.repeat(heights, dims[dim] // parts).reshape([-1 if axis == dim else 1 for axis in range(len(dims))])
    return gain


def gaussian(stream_key, shape, width, bound, pieces=(), kind=jnp.bfloat16):
    values = width * jax.random.normal(stream_key, shape, jnp.float32)
    if pieces:
        values = values * level_of(stream_key, shape, pieces, -0.22, 0.18)
    return jnp.clip(values, -bound, bound).astype(kind)


def setup_inputs(seed: int = 0) -> dict:
    streams_of = jax.random.split(jax.random.key(seed), 4)
    return {
        "jacobian": draw_jacobian(jax.random.fold_in(streams_of[3], 71), 0),
        "residual": gaussian(streams_of[1], (M,), 1.0, 6.0, ((0, 8),), jnp.float32),
        "damping": jnp.clip(jnp.exp(jax.random.uniform(streams_of[2], (1,), jnp.float32, math.log(0.3), math.log(3.0))), 0.3, 3.0),
    }


def reference(jacobian, residual, damping):
    gram = lax.dot_general(jacobian.astype(jnp.float32), jacobian.astype(jnp.float32), (((1,), (1,)), ((), ())), precision=lax.Precision.HIGHEST, preferred_element_type=jnp.float32)
    grad = jnp.dot(jacobian.astype(jnp.float32), residual.astype(jnp.float32), precision=lax.Precision.HIGHEST, preferred_element_type=jnp.float32)
    damped = gram + damping[0] * jnp.diag(jnp.diag(gram))
    factor = jnp.linalg.cholesky(damped)
    return -jax.scipy.linalg.cho_solve((factor, True), grad)
```

```python
import functools
import jax
import jax.numpy as jnp
from jax import lax
from jax.experimental import pallas as pl
from jax.experimental.pallas import tpu as pltpu
from jax.sharding import PartitionSpec as P

LANES = 128
MESH = pl.DeviceIdType.MESH
YS, CORES, ZS, XS = 4, 2, 8, 4


def regroup_kernel(j_ref, r_ref, out_ref, panel, pack, core_rx, y_rx, y_sum, z_rx, x_all, own_sem,
                   a2a_send, a2a_recv, core_send, core_recv, y_send, y_recv, z_send, z_recv, x_send, x_recv,
                   zg_send, zg_recv, yg_send, yg_recv, cg_send, cg_recv):
    sensor, space = lax.axis_index("sensor"), lax.axis_index("space")
    y, core = sensor // CORES, sensor % CORES
    z, x = space // XS, space % XS
    spaces = ZS * XS
    rows = j_ref.shape[0]
    cols = j_ref.shape[1] // spaces
    params = rows * spaces
    blocks = params // LANES

    def on_space(dz, dx):
        return lax.rem(z + dz + ZS, ZS) * XS + lax.rem(x + dx + XS, XS)

    def on_y(d):
        return lax.rem(y + d + YS, YS) * CORES + core

    other_core = y * CORES + (1 - core)

    own = pltpu.make_async_copy(
        j_ref.at[:, pl.ds(pl.multiple_of(space * cols, cols), cols)],
        panel.at[pl.ds(pl.multiple_of(space * rows, rows), rows), :],
        own_sem,
    )
    own.start()

    barrier = pltpu.get_barrier_semaphore()

    def greet(d, carry):
        pl.semaphore_signal(barrier, inc=1, device_id={"space": lax.rem(space + d, spaces)}, device_id_type=MESH)
        return carry

    lax.fori_loop(1, spaces, greet, 0)
    pl.semaphore_signal(barrier, inc=1, device_id={"sensor": other_core}, device_id_type=MESH)
    for d in range(1, YS):
        pl.semaphore_signal(barrier, inc=1, device_id={"sensor": on_y(d)}, device_id_type=MESH)
    pl.semaphore_wait(barrier, spaces - 1 + 1 + YS - 1)

    def regroup(d, sign):
        to = on_space(sign * (d // XS), sign * lax.rem(d, XS))
        src_of = to if sign == 1 else space
        at = space if sign == 1 else to
        return pltpu.make_async_remote_copy(
            src_ref=j_ref.at[:, pl.ds(pl.multiple_of(src_of * cols, cols), cols)],
            dst_ref=panel.at[pl.ds(pl.multiple_of(at * rows, rows), rows), :],
            send_sem=a2a_send.at[d],
            recv_sem=a2a_recv.at[at],
            device_id={"space": to},
            device_id_type=MESH,
        )

    def start(d, carry):
        regroup(d, 1).start()
        return carry

    def arrive(d, carry):
        regroup(d, -1).wait_recv()
        return carry

    def sent(d, carry):
        regroup(d, 1).wait_send()
        return carry

    lax.fori_loop(1, spaces, start, 0)
    pack[...] = jnp.zeros_like(pack)
    own.wait()
    lax.fori_loop(1, spaces, arrive, 0)

    high = lax.Precision.HIGHEST
    across = (((1,), (1,)), ((), ()))
    at = 0
    for b in range(blocks):
        left = panel[b * LANES : (b + 1) * LANES, :]
        strip = lax.dot_general(left, panel[b * LANES :, :], across, precision=high, preferred_element_type=jnp.float32)
        for c in range(blocks - b):
            pack[at : at + LANES, :] = strip[:, c * LANES : (c + 1) * LANES]
            at += LANES
    pieces = cols // LANES
    r_row = jnp.concatenate([r_ref[pl.ds(space * pieces + i, 1), :] for i in range(pieces)], axis=1)
    g = lax.dot_general(jnp.broadcast_to(r_row, (8, cols)), panel[...], across, precision=high, preferred_element_type=jnp.float32)
    for b in range(blocks):
        pack[at + b : at + b + 1, :] = g[0:1, b * LANES : (b + 1) * LANES]

    half = pack.shape[0] // CORES
    quarter = half // YS
    piece = quarter // ZS

    def remote(src, dst, send, recv, target):
        return pltpu.make_async_remote_copy(src_ref=src, dst_ref=dst, send_sem=send, recv_sem=recv, device_id=target, device_id_type=MESH)

    def run(copies):
        for c in copies:
            c.start()
        for c in copies:
            c.wait()

    mine = pl.multiple_of(core * half, half)
    theirs = pl.multiple_of((1 - core) * half, half)
    run([remote(pack.at[pl.ds(theirs, half), :], core_rx, core_send, core_recv, {"sensor": other_core})])
    pack[pl.ds(mine, half), :] += core_rx[...]

    def y_part(yy):
        return pl.ds(pl.multiple_of(mine + yy * quarter, quarter), quarter)

    run([
        remote(pack.at[y_part(lax.rem(y + d, YS)), :], y_rx.at[d - 1], y_send.at[d - 1], y_recv.at[d - 1], {"sensor": on_y(d)})
        for d in range(1, YS)
    ])
    y_sum[...] = pack[y_part(y), :] + y_rx[0] + y_rx[1] + y_rx[2]

    def z_part(zz, base=0):
        return pl.ds(pl.multiple_of(base + zz * piece, piece), piece)

    run([
        remote(y_sum.at[z_part(lax.rem(z + d, ZS)), :], z_rx.at[d - 1], z_send.at[d - 1], z_recv.at[d - 1], {"space": on_space(d, 0)})
        for d in range(1, ZS)
    ])
    total = y_sum[z_part(z), :]
    for d in range(ZS - 1):
        total = total + z_rx[d]
    x_all[x] = total
    run([
        remote(x_all.at[x], x_all.at[x], x_send.at[d - 1], x_recv.at[d - 1], {"space": on_space(0, d)})
        for d in range(1, XS)
    ])
    total = x_all[0]
    for d in range(1, XS):
        total = total + x_all[d]
    base = mine + y * quarter
    out_ref[z_part(z, base), :] = total
    run([
        remote(out_ref.at[z_part(z, base), :], out_ref.at[z_part(z, base), :], zg_send.at[d - 1], zg_recv.at[d - 1], {"space": on_space(d, 0)})
        for d in range(1, ZS)
    ])
    run([
        remote(out_ref.at[y_part(y), :], out_ref.at[y_part(y), :], yg_send.at[d - 1], yg_recv.at[d - 1], {"sensor": on_y(d)})
        for d in range(1, YS)
    ])
    run([remote(out_ref.at[pl.ds(mine, half), :], out_ref.at[pl.ds(mine, half), :], cg_send, cg_recv, {"sensor": other_core})])
    lax.fori_loop(1, spaces, sent, 0)


def normal_matrix(jacobian, residual):
    rows, local = jacobian.shape
    spaces = ZS * XS
    params, cols = rows * spaces, local // spaces
    blocks = params // LANES
    packed = (blocks * (blocks + 1) // 2 + 1) * LANES
    unit = CORES * YS * ZS * 8
    packed = -(-packed // unit) * unit
    half = packed // CORES
    quarter = half // YS
    piece = quarter // ZS
    f32, dma = jnp.float32, pltpu.SemaphoreType.DMA
    return pl.pallas_call(
        regroup_kernel,
        out_shape=jax.ShapeDtypeStruct((packed, LANES), f32),
        in_specs=[pl.BlockSpec(memory_space=pl.ANY), pl.BlockSpec(memory_space=pltpu.VMEM)],
        out_specs=pl.BlockSpec(memory_space=pltpu.VMEM),
        scratch_shapes=[
            pltpu.VMEM((params, cols), f32),
            pltpu.VMEM((packed, LANES), f32),
            pltpu.VMEM((half, LANES), f32),
            pltpu.VMEM((YS - 1, quarter, LANES), f32),
            pltpu.VMEM((quarter, LANES), f32),
            pltpu.VMEM((ZS - 1, piece, LANES), f32),
            pltpu.VMEM((XS, piece, LANES), f32),
            dma,
            dma((spaces,)), dma((spaces,)),
            dma, dma,
            dma((YS - 1,)), dma((YS - 1,)),
            dma((ZS - 1,)), dma((ZS - 1,)),
            dma((XS - 1,)), dma((XS - 1,)),
            dma((ZS - 1,)), dma((ZS - 1,)),
            dma((YS - 1,)), dma((YS - 1,)),
            dma, dma,
        ],
        compiler_params=pltpu.CompilerParams(collective_id=0, has_side_effects=True, vmem_limit_bytes=32 << 20),
    )(jacobian, residual.reshape(-1, LANES))


SLAB = 32


def block_at(b, c, blocks):
    return b * blocks - b * (b - 1) // 2 + (c - b)


def split3(v):
    hi = v.astype(jnp.bfloat16)
    rest = v - hi.astype(jnp.float32)
    mid = rest.astype(jnp.bfloat16)
    low = (rest - mid.astype(jnp.float32)).astype(jnp.bfloat16)
    return hi, mid, low


def solve_kernel(blocks, packed, damping, x_ref, mat):
    tri = blocks * (blocks + 1) // 2
    wide = blocks + 1
    eye = lax.broadcasted_iota(jnp.int32, (LANES, LANES), 0) == lax.broadcasted_iota(jnp.int32, (LANES, LANES), 1)
    lam = damping[0]
    scale_rows, scale_cols = [], []
    for b in range(blocks):
        at = block_at(b, b, blocks) * LANES
        diag = jnp.where(eye, packed[at : at + LANES, :], 0.0)
        scale_rows.append(lax.rsqrt(jnp.sum(diag, axis=0, keepdims=True)))
        scale_cols.append(lax.rsqrt(jnp.sum(diag, axis=1, keepdims=True)))
    for b in range(blocks):
        for c in range(b, blocks):
            at = block_at(b, c, blocks) * LANES
            v = packed[at : at + LANES, :] * scale_cols[b] * scale_rows[c]
            if b == c:
                v = jnp.where(eye, 1.0 + lam, v)
            mat[b * LANES : (b + 1) * LANES, c * LANES : (c + 1) * LANES] = v
        g_row = packed[tri * LANES + b : tri * LANES + b + 1, :] * scale_rows[b]
        g_col = jnp.sum(jnp.where(eye, g_row, 0.0), axis=1, keepdims=True)
        mat[b * LANES : (b + 1) * LANES, blocks * LANES :] = jnp.broadcast_to(g_col, (LANES, LANES))

    lane = lax.broadcasted_iota(jnp.int32, (8, LANES), 1)
    sub = lax.broadcasted_iota(jnp.int32, (8, LANES), 0)

    def row(v, i):
        return jnp.broadcast_to(v[i : i + 1, :], (8, LANES))

    def slab_step(b, inner):
        tiles = list(range(b, wide))
        top = b * LANES + inner * SLAB
        if not isinstance(top, int):
            top = pl.multiple_of(top, SLAB)
        groups = SLAB // 8
        s = [[mat[pl.ds(top + 8 * g, 8), t * LANES : (t + 1) * LANES] for t in tiles] for g in range(groups)]
        before = [[v for v in r] for r in s]
        for g in range(groups):
            shift = inner * SLAB + 8 * g
            rolled = [pltpu.roll(s[i][0], (LANES - shift) % LANES, 1) for i in range(groups)]
            cols = [[jnp.broadcast_to(rolled[i][:, q : q + 1], (8, LANES)) for q in range(8)] for i in range(groups)]
            for p in range(0, 8, 2):
                at, bt, ct = row(cols[g][p], p), row(cols[g][p + 1], p), row(cols[g][p + 1], p + 1)
                det = at * ct - bt * bt
                r = pl.reciprocal(det, approx=True)
                r = r * (2.0 - det * r)
                r = r * (2.0 - det * r)
                av, bv, cv = at * r, bt * r, ct * r

                def eliminate(z):
                    z0, z1 = row(z[g], p), row(z[g], p + 1)
                    u0 = cv * z0 - bv * z1
                    u1 = av * z1 - bv * z0
                    out = []
                    for i in range(groups):
                        v = z[i] - cols[i][p] * u0 - cols[i][p + 1] * u1
                        if i == g:
                            v = jnp.where(sub == p, u0, jnp.where(sub == p + 1, u1, v))
                        out.append(v)
                    return out

                for q in range(p + 2, 8):
                    new = eliminate([cols[i][q] for i in range(groups)])
                    for i in range(groups):
                        cols[i][q] = new[i]
                for t in range(len(tiles)):
                    new = eliminate([s[i][t] for i in range(groups)])
                    for i in range(groups):
                        s[i][t] = new[i]
        full = lambda a: jnp.concatenate([jnp.concatenate(r, axis=1) for r in a], axis=0)
        u = full(s)
        x = full(before)
        mat[pl.ds(top, SLAB), b * LANES :] = u
        keep = lax.broadcasted_iota(jnp.int32, x.shape, 1) >= (inner + 1) * SLAB
        x = jnp.where(keep, x, 0.0)
        xh, xm, xl = split3(x[:, : (blocks - b) * LANES])
        uh, um, ul = split3(u)
        left = jnp.concatenate([xh, xh, xm, xh, xl, xm], axis=0)
        right = jnp.concatenate([uh, um, uh, ul, uh, um], axis=0)
        for i in range(b, blocks):
            o = (i - b) * LANES
            prod = lax.dot_general(left[:, o : o + LANES], right[:, o:], (((0,), (0,)), ((), ())), preferred_element_type=jnp.float32)
            mat[i * LANES : (i + 1) * LANES, i * LANES :] -= prod

    for b in range(blocks):
        def body(inner, carry, b=b):
            slab_step(b, inner)
            return carry

        lax.fori_loop(0, LANES // SLAB, body, 0)

    per = LANES // SLAB
    xs = [jnp.zeros((1, LANES), jnp.float32) for _ in range(blocks)]
    for k in reversed(range(blocks * per)):
        b, inner = divmod(k, per)
        u = mat[k * SLAB : (k + 1) * SLAB, :]
        acc = None
        for t in range(b, blocks):
            if t == blocks - 1 and k == blocks * per - 1:
                continue
            term = u[:, t * LANES : (t + 1) * LANES] * xs[t]
            acc = term if acc is None else acc + term
        col = u[:, blocks * LANES :]
        if acc is not None:
            col = col - jnp.sum(acc, axis=1, keepdims=True)
        pick = lax.broadcasted_iota(jnp.int32, (SLAB, LANES), 1) == lax.broadcasted_iota(jnp.int32, (SLAB, LANES), 0) + inner * SLAB
        xs[b] = xs[b] + jnp.sum(jnp.where(pick, col, 0.0), axis=0, keepdims=True)
    for b in range(blocks):
        x_ref[b : b + 1, :] = -(xs[b] * scale_rows[b])


def solve(packed, damping, params):
    blocks = params // LANES
    out = pl.pallas_call(
        functools.partial(solve_kernel, blocks),
        out_shape=jax.ShapeDtypeStruct((blocks, LANES), jnp.float32),
        in_specs=[pl.BlockSpec(memory_space=pltpu.VMEM), pl.BlockSpec(memory_space=pltpu.SMEM)],
        out_specs=pl.BlockSpec(memory_space=pltpu.VMEM),
        scratch_shapes=[pltpu.VMEM((params, params + LANES), jnp.float32)],
        compiler_params=pltpu.CompilerParams(vmem_limit_bytes=32 << 20),
    )(packed, damping)
    return out.reshape(params)


def per_device(jacobian, residual, damping):
    params = jacobian.shape[0] * ZS * XS
    return solve(normal_matrix(jacobian, residual), damping, params)


def solution(mesh):
    placed = (P("space", "sensor"), P("sensor"), P())
    return jax.shard_map(per_device, mesh=mesh, in_specs=placed, out_specs=P(), check_vma=False)
```

```python
import functools
import jax
import jax.numpy as jnp
from jax import lax
from jax.experimental import pallas as pl
from jax.experimental.pallas import tpu as pltpu
from jax.sharding import PartitionSpec as P

LANES = 128
MESH = pl.DeviceIdType.MESH
YS, CORES, ZS, XS = 4, 2, 8, 4
CHUNKS = 4
SLAB = 64
PANEL = 16


def split3(v):
    hi = v.astype(jnp.bfloat16)
    rest = v - hi.astype(jnp.float32)
    mid = rest.astype(jnp.bfloat16)
    low = (rest - mid.astype(jnp.float32)).astype(jnp.bfloat16)
    return hi, mid, low


def regroup_kernel(j_ref, r_ref, out_ref, panel, r_own, pack, core_rx, y_rx, y_sum, z_rx, x_all, own_sem, r_sem,
                   a2a_send, a2a_recv, core_send, core_recv, y_send, y_recv, z_send, z_recv, x_send, x_recv,
                   zg_send, zg_recv, yg_send, yg_recv, cg_send, cg_recv):
    sensor, space = lax.axis_index("sensor"), lax.axis_index("space")
    y, core = sensor // CORES, sensor % CORES
    z, x = space // XS, space % XS
    spaces = ZS * XS
    rows = j_ref.shape[0]
    cols = j_ref.shape[1] // spaces
    params = rows * spaces
    blocks = params // LANES
    depth = cols // CHUNKS

    def on_space(dz, dx):
        return lax.rem(z + dz + ZS, ZS) * XS + lax.rem(x + dx + XS, XS)

    def on_y(d):
        return lax.rem(y + d + YS, YS) * CORES + core

    other_core = y * CORES + (1 - core)
    my_rows = pl.ds(pl.multiple_of(space * rows, rows), rows)

    def piece_of(device, chunk):
        return j_ref.at[:, pl.ds(pl.multiple_of(device * cols + chunk * depth, depth), depth)]

    own = [pltpu.make_async_copy(piece_of(space, c), panel.at[c, my_rows, :], own_sem.at[c]) for c in range(CHUNKS)]
    for copy in own:
        copy.start()
    r_copy = pltpu.make_async_copy(r_ref.at[space], r_own, r_sem)
    r_copy.start()

    barrier = pltpu.get_barrier_semaphore()

    def greet(d, carry):
        pl.semaphore_signal(barrier, inc=1, device_id={"space": lax.rem(space + d, spaces)}, device_id_type=MESH)
        return carry

    lax.fori_loop(1, spaces, greet, 0)
    pl.semaphore_signal(barrier, inc=1, device_id={"sensor": other_core}, device_id_type=MESH)
    for d in range(1, YS):
        pl.semaphore_signal(barrier, inc=1, device_id={"sensor": on_y(d)}, device_id_type=MESH)
    pl.semaphore_wait(barrier, spaces - 1 + 1 + YS - 1)

    for c in range(CHUNKS):

        def start(d, carry, c=c):
            to = on_space(d // XS, lax.rem(d, XS))
            pltpu.make_async_remote_copy(
                src_ref=piece_of(to, c),
                dst_ref=panel.at[c, my_rows, :],
                send_sem=a2a_send.at[c],
                recv_sem=a2a_recv.at[c],
                device_id={"space": to},
                device_id_type=MESH,
            ).start()
            return carry

        lax.fori_loop(1, spaces, start, 0)

    def all_of(c, sem):
        others = panel.at[c, pl.ds(0, params - rows), :]
        pltpu.make_async_copy(others, others, sem).wait()

    tri = blocks * (blocks + 1) // 2
    pack[tri * LANES :, :] = jnp.zeros((pack.shape[0] - tri * LANES, LANES), jnp.float32)
    across = (((1,), (1,)), ((), ()))
    r_copy.wait()
    for c in range(CHUNKS):
        own[c].wait()
        all_of(c, a2a_recv.at[c])
        hi, mid, low = split3(panel[c])
        left = jnp.concatenate([hi, hi, mid, hi, low, mid], axis=1)
        right = jnp.concatenate([hi, mid, hi, low, hi, mid], axis=1)
        at = 0
        for b in range(blocks):
            strip = lax.dot_general(left[b * LANES : (b + 1) * LANES, :], right[b * LANES :, :], across, preferred_element_type=jnp.float32)
            for k in range(blocks - b):
                block = strip[:, k * LANES : (k + 1) * LANES]
                pack[at : at + LANES, :] = block if c == 0 else pack[at : at + LANES, :] + block
                at += LANES
        pieces = depth // LANES
        r_row = jnp.concatenate([r_own[c * pieces + i : c * pieces + i + 1, :] for i in range(pieces)], axis=1)
        rh, rm, rl = split3(jnp.broadcast_to(r_row, (16, depth)))
        r_left = jnp.concatenate([rh, rh, rm, rh, rl, rm], axis=1)
        g = lax.dot_general(r_left, right, across, preferred_element_type=jnp.float32)
        for b in range(blocks):
            pack[at + b : at + b + 1, :] += g[0:1, b * LANES : (b + 1) * LANES]

    half = pack.shape[0] // CORES
    quarter = half // YS
    piece = quarter // ZS

    def remote(src, dst, send, recv, target):
        return pltpu.make_async_remote_copy(src_ref=src, dst_ref=dst, send_sem=send, recv_sem=recv, device_id=target, device_id_type=MESH)

    def run(copies):
        for copy in copies:
            copy.start()
        for copy in copies:
            copy.wait()

    mine = pl.multiple_of(core * half, half)
    theirs = pl.multiple_of((1 - core) * half, half)

    def y_part(yy, base):
        return pl.ds(pl.multiple_of(base + yy * quarter, quarter), quarter)

    def z_part(zz, base=0):
        return pl.ds(pl.multiple_of(base + zz * piece, piece), piece)

    order = (2, 1, 3, 0)
    core_copies = {}
    for d in order:
        yy = lax.rem(y + d, YS)
        core_copies[d] = remote(pack.at[y_part(yy, theirs), :], core_rx.at[d], core_send.at[d], core_recv.at[d], {"sensor": other_core})
        core_copies[d].start()
    y_copies = []
    for d in order:
        part = y_part(lax.rem(y + d, YS), mine)
        core_copies[d].wait_recv()
        if d:
            pack[part, :] += core_rx[d]
            y_copies.append(remote(pack.at[part, :], y_rx.at[d - 1], y_send.at[d - 1], y_recv.at[d - 1], {"sensor": on_y(d)}))
            y_copies[-1].start()
        else:
            y_sum[...] = pack[part, :] + core_rx[d]
    for copy in y_copies:
        copy.wait_recv()
    y_sum[...] += y_rx[0] + y_rx[1] + y_rx[2]

    z_copies = [
        remote(y_sum.at[z_part(lax.rem(z + d, ZS)), :], z_rx.at[d - 1], z_send.at[d - 1], z_recv.at[d - 1], {"space": on_space(d, 0)})
        for d in (4, 3, 5, 2, 6, 1, 7)
    ]
    for copy in z_copies:
        copy.start()
    for copy in z_copies:
        copy.wait_recv()
    total = y_sum[z_part(z), :]
    for d in range(ZS - 1):
        total = total + z_rx[d]
    x_all[x] = total
    x_copies = [
        remote(x_all.at[x], x_all.at[x], x_send.at[d - 1], x_recv.at[d - 1], {"space": on_space(0, d)})
        for d in (2, 1, 3)
    ]
    for copy in x_copies:
        copy.start()
    for copy in x_copies:
        copy.wait_recv()
    total = x_all[0]
    for d in range(1, XS):
        total = total + x_all[d]
    base = mine + y * quarter
    done = out_ref.at[z_part(z, base), :]
    done[...] = total
    zg_copies = [
        remote(done, done, zg_send.at[d - 1], zg_recv.at[d - 1], {"space": on_space(d, 0)})
        for d in (4, 3, 5, 2, 6, 1, 7)
    ]
    for copy in zg_copies:
        copy.start()
    for copy in zg_copies:
        copy.wait_recv()
    mine_done = out_ref.at[y_part(y, mine), :]
    yg_copies = {d: remote(mine_done, mine_done, yg_send.at[d - 1], yg_recv.at[d - 1], {"sensor": on_y(d)}) for d in (2, 1, 3)}
    for copy in yg_copies.values():
        copy.start()
    cg_copies = []
    for d in (0, 1, 3, 2):
        if d:
            yg_copies[d].wait_recv()
        got = out_ref.at[y_part(lax.rem(y - d + YS, YS), mine), :]
        cg_copies.append(remote(got, got, cg_send.at[d], cg_recv.at[d], {"sensor": other_core}))
        cg_copies[-1].start()
    for copy in cg_copies:
        copy.wait_recv()
    for copy in (*core_copies.values(), *y_copies, *z_copies, *x_copies, *zg_copies, *yg_copies.values(), *cg_copies):
        copy.wait_send()
    for c in range(CHUNKS):
        all_of(c, a2a_send.at[c])


def normal_matrix(jacobian, residual):
    rows, local = jacobian.shape
    spaces = ZS * XS
    params, cols = rows * spaces, local // spaces
    blocks = params // LANES
    packed = (blocks * (blocks + 1) // 2 + 1) * LANES
    unit = CORES * YS * ZS * 8
    packed = -(-packed // unit) * unit
    half = packed // CORES
    quarter = half // YS
    piece = quarter // ZS
    f32, dma = jnp.float32, pltpu.SemaphoreType.DMA
    return pl.pallas_call(
        regroup_kernel,
        out_shape=jax.ShapeDtypeStruct((packed, LANES), f32),
        in_specs=[pl.BlockSpec(memory_space=pltpu.HBM), pl.BlockSpec(memory_space=pltpu.HBM)],
        out_specs=pl.BlockSpec(memory_space=pltpu.VMEM),
        scratch_shapes=[
            pltpu.VMEM((CHUNKS, params, cols // CHUNKS), f32),
            pltpu.VMEM((cols // LANES, LANES), f32),
            pltpu.VMEM((packed, LANES), f32),
            pltpu.VMEM((YS, quarter, LANES), f32),
            pltpu.VMEM((YS - 1, quarter, LANES), f32),
            pltpu.VMEM((quarter, LANES), f32),
            pltpu.VMEM((ZS - 1, piece, LANES), f32),
            pltpu.VMEM((XS, piece, LANES), f32),
            dma((CHUNKS,)), dma,
            dma((CHUNKS,)), dma((CHUNKS,)),
            dma((YS,)), dma((YS,)),
            dma((YS - 1,)), dma((YS - 1,)),
            dma((ZS - 1,)), dma((ZS - 1,)),
            dma((XS - 1,)), dma((XS - 1,)),
            dma((ZS - 1,)), dma((ZS - 1,)),
            dma((YS - 1,)), dma((YS - 1,)),
            dma((YS,)), dma((YS,)),
        ],
        compiler_params=pltpu.CompilerParams(collective_id=0, has_side_effects=True, vmem_limit_bytes=58 << 20),
    )(jacobian, residual.reshape(spaces, -1, LANES))


def block_at(b, c, blocks):
    return b * blocks - b * (b - 1) // 2 + (c - b)


def solve_kernel(blocks, packed, damping, x_ref, mat):
    tri = blocks * (blocks + 1) // 2
    wide = blocks + 1
    eye = lax.broadcasted_iota(jnp.int32, (LANES, LANES), 0) == lax.broadcasted_iota(jnp.int32, (LANES, LANES), 1)
    lam = damping[0]
    scale_rows, scale_cols = [], []
    for b in range(blocks):
        at = block_at(b, b, blocks) * LANES
        diag = jnp.where(eye, packed[at : at + LANES, :], 0.0)
        scale_rows.append(lax.rsqrt(jnp.sum(diag, axis=0, keepdims=True)))
        scale_cols.append(lax.rsqrt(jnp.sum(diag, axis=1, keepdims=True)))
    for b in range(blocks):
        for c in range(b, blocks):
            at = block_at(b, c, blocks) * LANES
            v = packed[at : at + LANES, :] * scale_cols[b] * scale_rows[c]
            if b == c:
                v = jnp.where(eye, 1.0 + lam, v)
            mat[b * LANES : (b + 1) * LANES, c * LANES : (c + 1) * LANES] = v
        g_row = packed[tri * LANES + b : tri * LANES + b + 1, :] * scale_rows[b]
        g_col = jnp.sum(jnp.where(eye, g_row, 0.0), axis=1, keepdims=True)
        mat[b * LANES : (b + 1) * LANES, blocks * LANES :] = jnp.broadcast_to(g_col, (LANES, LANES))

    lane = lax.broadcasted_iota(jnp.int32, (8, LANES), 1)
    sub = lax.broadcasted_iota(jnp.int32, (8, LANES), 0)

    def row(v, i):
        return jnp.broadcast_to(v[i : i + 1, :], (8, LANES))

    def invert(t, own):
        wide_by = PANEL // 8
        for h in range(SLAB // PANEL):
            mine = range(h * wide_by, (h + 1) * wide_by)
            first = own + h * PANEL

            def column(v, q):
                return jnp.broadcast_to(v[:, first + q : first + q + 1], (8, LANES))

            cols = [[column(t[i], q) for i in mine] for q in range(PANEL)]
            rows_of = [t[i] for i in mine]
            for p in range(0, PANEL, 2):
                g, k = divmod(p, 8)
                at, bt, ct = row(cols[p][g], k), row(cols[p + 1][g], k), row(cols[p + 1][g], k + 1)
                r = pltpu.reciprocal(at * ct - bt * bt, approx=True)
                if p == 0:
                    tie = r * 0.0
                av, bv, cv = at * r, bt * r, ct * r
                left, right = list(cols[p]), list(cols[p + 1])
                left[g] = left[g] - jnp.where(sub == k, 1.0, 0.0)
                right[g] = right[g] - jnp.where(sub == k + 1, 1.0, 0.0)
                by0 = [x * cv - y * bv for x, y in zip(left, right)]
                by1 = [y * av - x * bv for x, y in zip(left, right)]

                def eliminate(z):
                    z0, z1 = row(z[g], k), row(z[g], k + 1)
                    return [v - (x * z0 + y * z1) for v, x, y in zip(z, by0, by1)]

                for q in range(p + 2, PANEL):
                    cols[q] = eliminate(cols[q])
                rows_of = eliminate(rows_of)
            u_rows = [row(rows_of[q // 8], q % 8) for q in range(PANEL)]
            others = {i: t[i] + tie for i in range(SLAB // 8) if i not in mine}
            parts = {i: [] for i in others}
            for q in range(PANEL):
                for i in others:
                    parts[i].append(column(others[i], q) * u_rows[q])
            new = []
            for i in range(SLAB // 8):
                if i in mine:
                    new.append(rows_of[i - mine[0]])
                    continue
                while len(parts[i]) > 1:
                    parts[i] = [x + y for x, y in zip(parts[i][::2], parts[i][1::2])]
                new.append(t[i] - parts[i][0])
            t = new
        return t

    def slab_step(b, inner):
        top = b * LANES + inner * SLAB
        own = inner * SLAB
        rest = LANES - SLAB - own
        s = mat[top : top + SLAB, b * LANES :]
        t = []
        for i in range(SLAB // 8):
            unit = jnp.where(lane == sub + (rest + 8 * i), 1.0, 0.0)
            t.append(jnp.where((lane >= own) & (lane < own + SLAB), s[8 * i : 8 * i + 8, :LANES], unit))
        inv = jnp.concatenate(invert(t, own), axis=0)
        skip = LANES if inner else 0
        sh, sm, sl = split3(s[:, skip:])
        ih, im, il = split3(inv)
        weights = jnp.concatenate([ih, ih, im, ih, il, im], axis=0)
        stack = jnp.concatenate([sh, sm, sh, sl, sh, sm], axis=0)
        over = (((0,), (0,)), ((), ()))
        u = lax.dot_general(weights, stack, over, preferred_element_type=jnp.float32)[rest : rest + SLAB, :]
        mat[top : top + SLAB, b * LANES + skip :] = u
        count = (blocks - b) * LANES - skip
        if count == 0:
            return

        def later(v):
            v = v[:, :count]
            if inner:
                return v
            edge = jnp.where(lax.broadcasted_iota(jnp.int32, (SLAB, LANES), 1) >= SLAB, v[:, :LANES], jnp.zeros((SLAB, LANES), v.dtype))
            return edge if count == LANES else jnp.concatenate([edge, v[:, LANES:]], axis=1)

        xh, xm, xl = later(sh), later(sm), later(sl)
        uh, um, ul = split3(u)
        left = jnp.concatenate([xh, xh, xm, xh, xl, xm], axis=0)
        right = jnp.concatenate([uh, um, uh, ul, uh, um], axis=0)
        for o in range(0, count, LANES):
            at = b * LANES + skip + o
            prod = lax.dot_general(left[:, o : o + LANES], right[:, o:], over, preferred_element_type=jnp.float32)
            mat[at : at + LANES, at:] -= prod

    for b in range(blocks):
        for inner in range(LANES // SLAB):
            slab_step(b, inner)

    per = LANES // SLAB
    xs = [jnp.zeros((1, LANES), jnp.float32) for _ in range(blocks)]
    for k in reversed(range(blocks * per)):
        b, inner = divmod(k, per)
        u = mat[k * SLAB : (k + 1) * SLAB, :]
        acc = None
        for t in range(b + (inner == per - 1), blocks):
            term = u[:, t * LANES : (t + 1) * LANES] * xs[t]
            acc = term if acc is None else acc + term
        col = u[:, blocks * LANES :]
        if acc is not None:
            col = col - jnp.sum(acc, axis=1, keepdims=True)
        pick = lax.broadcasted_iota(jnp.int32, (SLAB, LANES), 1) == lax.broadcasted_iota(jnp.int32, (SLAB, LANES), 0) + inner * SLAB
        xs[b] = xs[b] + jnp.sum(jnp.where(pick, col, 0.0), axis=0, keepdims=True)
    for b in range(blocks):
        x_ref[b : b + 1, :] = -(xs[b] * scale_rows[b])


def solve(packed, damping, params):
    blocks = params // LANES
    out = pl.pallas_call(
        functools.partial(solve_kernel, blocks),
        out_shape=jax.ShapeDtypeStruct((blocks, LANES), jnp.float32),
        in_specs=[pl.BlockSpec(memory_space=pltpu.VMEM), pl.BlockSpec(memory_space=pltpu.SMEM)],
        out_specs=pl.BlockSpec(memory_space=pltpu.VMEM),
        scratch_shapes=[pltpu.VMEM((params, params + LANES), jnp.float32)],
        compiler_params=pltpu.CompilerParams(vmem_limit_bytes=58 << 20),
    )(packed, damping)
    return out.reshape(params)


def per_device(jacobian, residual, damping):
    params = jacobian.shape[0] * ZS * XS
    return solve(normal_matrix(jacobian, residual), damping, params)


def solution(mesh):
    placed = (P("space", "sensor"), P("sensor"), P())
    return jax.shard_map(per_device, mesh=mesh, in_specs=placed, out_specs=P(), check_vma=False)
```

```python
import functools
import jax
import jax.numpy as jnp
from jax import lax
from jax.experimental import pallas as pl
from jax.experimental.pallas import tpu as pltpu
from jax.sharding import PartitionSpec as P

LANES = 128
MESH = pl.DeviceIdType.MESH
YS, CORES, ZS, XS = 4, 2, 8, 4
CHUNKS = 4
SLAB = 64
PANEL = 16


def split3(v):
    hi = v.astype(jnp.bfloat16)
    rest = v - hi.astype(jnp.float32)
    mid = rest.astype(jnp.bfloat16)
    low = (rest - mid.astype(jnp.float32)).astype(jnp.bfloat16)
    return hi, mid, low


def regroup_kernel(j_ref, r_ref, out_ref, panel, r_own, pack, core_rx, plane_rx, z_all, own_sem, r_sem,
                   a2a_send, a2a_recv, core_send, core_recv, plane_send, plane_recv, z_send, z_recv,
                   back_send, back_recv, last_send, last_recv):
    sensor, space = lax.axis_index("sensor"), lax.axis_index("space")
    y, core = sensor // CORES, sensor % CORES
    z, x = space // XS, space % XS
    spaces = ZS * XS
    rows = j_ref.shape[0]
    cols = j_ref.shape[1] // spaces
    params = rows * spaces
    blocks = params // LANES
    depth = cols // CHUNKS

    def on_space(dz, dx):
        return lax.rem(z + dz + ZS, ZS) * XS + lax.rem(x + dx + XS, XS)

    def in_plane(dy, dx):
        return {"sensor": lax.rem(y + dy, YS) * CORES + core, "space": on_space(0, dx)}

    other_core = y * CORES + (1 - core)
    my_rows = pl.ds(pl.multiple_of(space * rows, rows), rows)

    def piece_of(device, chunk):
        return j_ref.at[:, pl.ds(pl.multiple_of(device * cols + chunk * depth, depth), depth)]

    own = [pltpu.make_async_copy(piece_of(space, c), panel.at[c, my_rows, :], own_sem.at[c]) for c in range(CHUNKS)]
    for copy in own:
        copy.start()
    r_copy = pltpu.make_async_copy(r_ref.at[space], r_own, r_sem)
    r_copy.start()

    barrier = pltpu.get_barrier_semaphore()

    def greet(d, carry):
        pl.semaphore_signal(barrier, inc=1, device_id={"space": lax.rem(space + d, spaces)}, device_id_type=MESH)
        return carry

    lax.fori_loop(1, spaces, greet, 0)
    pl.semaphore_signal(barrier, inc=1, device_id={"sensor": other_core}, device_id_type=MESH)
    for dy in range(1, YS):
        for dx in range(XS):
            pl.semaphore_signal(barrier, inc=1, device_id=in_plane(dy, dx), device_id_type=MESH)
    pl.semaphore_wait(barrier, spaces - 1 + 1 + (YS - 1) * XS)

    for c in range(CHUNKS):

        def start(d, carry, c=c):
            to = on_space(d // XS, lax.rem(d, XS))
            pltpu.make_async_remote_copy(
                src_ref=piece_of(to, c),
                dst_ref=panel.at[c, my_rows, :],
                send_sem=a2a_send.at[c],
                recv_sem=a2a_recv.at[c],
                device_id={"space": to},
                device_id_type=MESH,
            ).start()
            return carry

        lax.fori_loop(1, spaces, start, 0)

    def all_of(c, sem):
        others = panel.at[c, pl.ds(0, params - rows), :]
        pltpu.make_async_copy(others, others, sem).wait()

    tri = blocks * (blocks + 1) // 2
    pack[tri * LANES :, :] = jnp.zeros((pack.shape[0] - tri * LANES, LANES), jnp.float32)
    across = (((1,), (1,)), ((), ()))
    r_copy.wait()
    for c in range(CHUNKS):
        own[c].wait()
        all_of(c, a2a_recv.at[c])
        hi, mid, low = split3(panel[c])
        left = jnp.concatenate([hi, hi, mid, hi, low, mid], axis=1)
        right = jnp.concatenate([hi, mid, hi, low, hi, mid], axis=1)
        at = 0
        for b in range(blocks):
            strip = lax.dot_general(left[b * LANES : (b + 1) * LANES, :], right[b * LANES :, :], across, preferred_element_type=jnp.float32)
            for k in range(blocks - b):
                block = strip[:, k * LANES : (k + 1) * LANES]
                pack[at : at + LANES, :] = block if c == 0 else pack[at : at + LANES, :] + block
                at += LANES
        pieces = depth // LANES
        r_row = jnp.concatenate([r_own[c * pieces + i : c * pieces + i + 1, :] for i in range(pieces)], axis=1)
        rh, rm, rl = split3(jnp.broadcast_to(r_row, (16, depth)))
        r_left = jnp.concatenate([rh, rh, rm, rh, rl, rm], axis=1)
        g = lax.dot_general(r_left, right, across, preferred_element_type=jnp.float32)
        for b in range(blocks):
            pack[at + b : at + b + 1, :] += g[0:1, b * LANES : (b + 1) * LANES]

    half = pack.shape[0] // CORES
    strip = half // YS
    piece = strip // XS

    def remote(src, dst, send, recv, target):
        return pltpu.make_async_remote_copy(src_ref=src, dst_ref=dst, send_sem=send, recv_sem=recv, device_id=target, device_id_type=MESH)

    mine = pl.multiple_of(core * half, half)
    theirs = pl.multiple_of((1 - core) * half, half)

    def strip_of(yy, base):
        return pl.ds(pl.multiple_of(base + yy * strip, strip), strip)

    def piece_at(yy, xx):
        return pl.ds(pl.multiple_of(mine + yy * strip + xx * piece, piece), piece)

    sent = []
    order = (2, 1, 3, 0)
    core_copies = {}
    for dy in order:
        core_copies[dy] = remote(pack.at[strip_of(lax.rem(y + dy, YS), theirs), :], core_rx.at[dy], core_send.at[dy], core_recv.at[dy], {"sensor": other_core})
        core_copies[dy].start()
    sent += core_copies.values()
    plane = []
    for dy in order:
        to_y = lax.rem(y + dy, YS)
        core_copies[dy].wait_recv()
        pack[strip_of(to_y, mine), :] += core_rx[dy]
        for dx in order:
            if dy or dx:
                k = dy * XS + dx - 1
                plane.append(remote(pack.at[piece_at(to_y, lax.rem(x + dx, XS)), :], plane_rx.at[k], plane_send.at[k], plane_recv.at[k], in_plane(dy, dx)))
                plane[-1].start()
    sent += plane
    for copy in plane:
        copy.wait_recv()
    parts = [pack[piece_at(y, x), :]] + [plane_rx[k] for k in range(YS * XS - 1)]

    def add_up(parts):
        while len(parts) > 1:
            parts = [u + v for u, v in zip(parts[::2], parts[1::2])]
        return parts[0]

    z_all[z] = add_up(parts)
    z_copies = [
        remote(z_all.at[z], z_all.at[z], z_send.at[d - 1], z_recv.at[d - 1], {"space": on_space(d, 0)})
        for d in (4, 3, 5, 2, 6, 1, 7)
    ]
    for copy in z_copies:
        copy.start()
    sent += z_copies
    for copy in z_copies:
        copy.wait_recv()
    done = out_ref.at[piece_at(y, x), :]
    done[...] = add_up([z_all[i] for i in range(ZS)])
    back = {}
    for dy in order:
        for dx in order:
            if dy or dx:
                k = dy * XS + dx - 1
                back[dy, dx] = remote(done, done, back_send.at[k], back_recv.at[k], in_plane(dy, dx))
                back[dy, dx].start()
    sent += back.values()
    last = []
    for dy in (0, 1, 3, 2):
        for dx in order:
            if dy or dx:
                back[dy, dx].wait_recv()
        got = out_ref.at[strip_of(lax.rem(y - dy + YS, YS), mine), :]
        last.append(remote(got, got, last_send.at[dy], last_recv.at[dy], {"sensor": other_core}))
        last[-1].start()
    sent += last
    for copy in last:
        copy.wait_recv()
    for copy in sent:
        copy.wait_send()
    for c in range(CHUNKS):
        all_of(c, a2a_send.at[c])


def normal_matrix(jacobian, residual):
    rows, local = jacobian.shape
    spaces = ZS * XS
    params, cols = rows * spaces, local // spaces
    blocks = params // LANES
    packed = (blocks * (blocks + 1) // 2 + 1) * LANES
    unit = CORES * YS * XS * 8
    packed = -(-packed // unit) * unit
    half = packed // CORES
    strip = half // YS
    piece = strip // XS
    f32, dma = jnp.float32, pltpu.SemaphoreType.DMA
    return pl.pallas_call(
        regroup_kernel,
        out_shape=jax.ShapeDtypeStruct((packed, LANES), f32),
        in_specs=[pl.BlockSpec(memory_space=pl.ANY), pl.BlockSpec(memory_space=pl.ANY)],
        out_specs=pl.BlockSpec(memory_space=pltpu.VMEM),
        scratch_shapes=[
            pltpu.VMEM((CHUNKS, params, cols // CHUNKS), f32),
            pltpu.VMEM((cols // LANES, LANES), f32),
            pltpu.VMEM((packed, LANES), f32),
            pltpu.VMEM((YS, strip, LANES), f32),
            pltpu.VMEM((YS * XS - 1, piece, LANES), f32),
            pltpu.VMEM((ZS, piece, LANES), f32),
            dma((CHUNKS,)), dma,
            dma((CHUNKS,)), dma((CHUNKS,)),
            dma((YS,)), dma((YS,)),
            dma((YS * XS - 1,)), dma((YS * XS - 1,)),
            dma((ZS - 1,)), dma((ZS - 1,)),
            dma((YS * XS - 1,)), dma((YS * XS - 1,)),
            dma((YS,)), dma((YS,)),
        ],
        compiler_params=pltpu.CompilerParams(collective_id=0, has_side_effects=True, vmem_limit_bytes=58 << 20),
    )(jacobian, residual.reshape(spaces, -1, LANES))


def block_at(b, c, blocks):
    return b * blocks - b * (b - 1) // 2 + (c - b)


def solve_kernel(blocks, packed, damping, x_ref, mat):
    tri = blocks * (blocks + 1) // 2
    wide = blocks + 1
    eye = lax.broadcasted_iota(jnp.int32, (LANES, LANES), 0) == lax.broadcasted_iota(jnp.int32, (LANES, LANES), 1)
    lam = damping[0]
    scale_rows, scale_cols = [], []
    for b in range(blocks):
        at = block_at(b, b, blocks) * LANES
        diag = jnp.where(eye, packed[at : at + LANES, :], 0.0)
        scale_rows.append(lax.rsqrt(jnp.sum(diag, axis=0, keepdims=True)))
        scale_cols.append(lax.rsqrt(jnp.sum(diag, axis=1, keepdims=True)))
    for b in range(blocks):
        for c in range(b, blocks):
            at = block_at(b, c, blocks) * LANES
            v = packed[at : at + LANES, :] * scale_cols[b] * scale_rows[c]
            if b == c:
                v = jnp.where(eye, 1.0 + lam, v)
            mat[b * LANES : (b + 1) * LANES, c * LANES : (c + 1) * LANES] = v
        g_row = packed[tri * LANES + b : tri * LANES + b + 1, :] * scale_rows[b]
        g_col = jnp.sum(jnp.where(eye, g_row, 0.0), axis=1, keepdims=True)
        mat[b * LANES : (b + 1) * LANES, blocks * LANES :] = jnp.broadcast_to(g_col, (LANES, LANES))

    lane = lax.broadcasted_iota(jnp.int32, (8, LANES), 1)
    sub = lax.broadcasted_iota(jnp.int32, (8, LANES), 0)

    def row(v, i):
        return jnp.broadcast_to(v[i : i + 1, :], (8, LANES))

    def invert(t, own):
        wide_by = PANEL // 8
        for h in range(SLAB // PANEL):
            mine = range(h * wide_by, (h + 1) * wide_by)
            first = own + h * PANEL

            def column(v, q):
                return jnp.broadcast_to(v[:, first + q : first + q + 1], (8, LANES))

            cols = [[column(t[i], q) for i in mine] for q in range(PANEL)]
            rows_of = [t[i] for i in mine]
            for p in range(0, PANEL, 2):
                g, k = divmod(p, 8)
                at, bt, ct = row(cols[p][g], k), row(cols[p + 1][g], k), row(cols[p + 1][g], k + 1)
                r = pltpu.reciprocal(at * ct - bt * bt, approx=True)
                if p == 0:
                    tie = r * 0.0
                av, bv, cv = at * r, bt * r, ct * r
                left, right = list(cols[p]), list(cols[p + 1])
                left[g] = left[g] - jnp.where(sub == k, 1.0, 0.0)
                right[g] = right[g] - jnp.where(sub == k + 1, 1.0, 0.0)
                by0 = [x * cv - y * bv for x, y in zip(left, right)]
                by1 = [y * av - x * bv for x, y in zip(left, right)]

                def eliminate(z):
                    z0, z1 = row(z[g], k), row(z[g], k + 1)
                    return [v - (x * z0 + y * z1) for v, x, y in zip(z, by0, by1)]

                for q in range(p + 2, PANEL):
                    cols[q] = eliminate(cols[q])
                rows_of = eliminate(rows_of)
            u_rows = [row(rows_of[q // 8], q % 8) for q in range(PANEL)]
            others = {i: t[i] + tie for i in range(SLAB // 8) if i not in mine}
            parts = {i: [] for i in others}
            for q in range(PANEL):
                for i in others:
                    parts[i].append(column(others[i], q) * u_rows[q])
            new = []
            for i in range(SLAB // 8):
                if i in mine:
                    new.append(rows_of[i - mine[0]])
                    continue
                while len(parts[i]) > 1:
                    parts[i] = [x + y for x, y in zip(parts[i][::2], parts[i][1::2])]
                new.append(t[i] - parts[i][0])
            t = new
        return t

    def slab_step(b, inner):
        top = b * LANES + inner * SLAB
        own = inner * SLAB
        rest = LANES - SLAB - own
        s = mat[top : top + SLAB, b * LANES :]
        t = []
        for i in range(SLAB // 8):
            unit = jnp.where(lane == sub + (rest + 8 * i), 1.0, 0.0)
            t.append(jnp.where((lane >= own) & (lane < own + SLAB), s[8 * i : 8 * i + 8, :LANES], unit))
        inv = jnp.concatenate(invert(t, own), axis=0)
        skip = LANES if inner else 0
        sh, sm, sl = split3(s[:, skip:])
        ih, im, il = split3(inv)
        weights = jnp.concatenate([ih, ih, im, ih, il, im], axis=0)
        stack = jnp.concatenate([sh, sm, sh, sl, sh, sm], axis=0)
        over = (((0,), (0,)), ((), ()))
        u = lax.dot_general(weights, stack, over, preferred_element_type=jnp.float32)[rest : rest + SLAB, :]
        mat[top : top + SLAB, b * LANES + skip :] = u
        count = (blocks - b) * LANES - skip
        if count == 0:
            return

        def later(v):
            v = v[:, :count]
            if inner:
                return v
            edge = jnp.where(lax.broadcasted_iota(jnp.int32, (SLAB, LANES), 1) >= SLAB, v[:, :LANES], jnp.zeros((SLAB, LANES), v.dtype))
            return edge if count == LANES else jnp.concatenate([edge, v[:, LANES:]], axis=1)

        xh, xm, xl = later(sh), later(sm), later(sl)
        uh, um, ul = split3(u)
        left = jnp.concatenate([xh, xh, xm, xh, xl, xm], axis=0)
        right = jnp.concatenate([uh, um, uh, ul, uh, um], axis=0)
        for o in range(0, count, LANES):
            at = b * LANES + skip + o
            prod = lax.dot_general(left[:, o : o + LANES], right[:, o:], over, preferred_element_type=jnp.float32)
            mat[at : at + LANES, at:] -= prod

    for b in range(blocks):
        for inner in range(LANES // SLAB):
            slab_step(b, inner)

    per = LANES // SLAB
    xs = [jnp.zeros((1, LANES), jnp.float32) for _ in range(blocks)]
    for k in reversed(range(blocks * per)):
        b, inner = divmod(k, per)
        u = mat[k * SLAB : (k + 1) * SLAB, :]
        acc = None
        for t in range(b + (inner == per - 1), blocks):
            term = u[:, t * LANES : (t + 1) * LANES] * xs[t]
            acc = term if acc is None else acc + term
        col = u[:, blocks * LANES :]
        if acc is not None:
            col = col - jnp.sum(acc, axis=1, keepdims=True)
        pick = lax.broadcasted_iota(jnp.int32, (SLAB, LANES), 1) == lax.broadcasted_iota(jnp.int32, (SLAB, LANES), 0) + inner * SLAB
        xs[b] = xs[b] + jnp.sum(jnp.where(pick, col, 0.0), axis=0, keepdims=True)
    for b in range(blocks):
        x_ref[b : b + 1, :] = -(xs[b] * scale_rows[b])


def solve(packed, damping, params):
    blocks = params // LANES
    out = pl.pallas_call(
        functools.partial(solve_kernel, blocks),
        out_shape=jax.ShapeDtypeStruct((blocks, LANES), jnp.float32),
        in_specs=[pl.BlockSpec(memory_space=pltpu.VMEM), pl.BlockSpec(memory_space=pltpu.SMEM)],
        out_specs=pl.BlockSpec(memory_space=pltpu.VMEM),
        scratch_shapes=[pltpu.VMEM((params, params + LANES), jnp.float32)],
        compiler_params=pltpu.CompilerParams(vmem_limit_bytes=58 << 20),
    )(packed, damping)
    return out.reshape(params)


def per_device(jacobian, residual, damping):
    params = jacobian.shape[0] * ZS * XS
    return solve(normal_matrix(jacobian, residual), damping, params)


def solution(mesh):
    placed = (P("space", "sensor"), P("sensor"), P())
    return jax.shard_map(per_device, mesh=mesh, in_specs=placed, out_specs=P(), check_vma=False)
```

```python
import functools
import jax
import jax.numpy as jnp
from jax import lax
from jax.experimental import pallas as pl
from jax.experimental.pallas import tpu as pltpu
from jax.sharding import PartitionSpec as P

LANES = 128
MESH = pl.DeviceIdType.MESH
YS, CORES, ZS, XS = 4, 2, 8, 4
CHUNKS = 4
WAVES = 2
SLAB = 64
PANEL = 16


def split3(v):
    hi = v.astype(jnp.bfloat16)
    rest = v - hi.astype(jnp.float32)
    mid = rest.astype(jnp.bfloat16)
    low = (rest - mid.astype(jnp.float32)).astype(jnp.bfloat16)
    return hi, mid, low


def regroup_kernel(j_ref, r_ref, out_ref, panel, r_own, pack, core_rx, plane_rx, z_all, own_sem, r_sem,
                   a2a_send, a2a_recv, core_send, core_recv, plane_send, plane_recv, z_send, z_recv,
                   back_send, back_recv, last_send, last_recv):
    sensor, space = lax.axis_index("sensor"), lax.axis_index("space")
    y, core = sensor // CORES, sensor % CORES
    z, x = space // XS, space % XS
    spaces = ZS * XS
    rows = j_ref.shape[0]
    cols = j_ref.shape[1] // spaces
    params = rows * spaces
    blocks = params // LANES
    depth = cols // CHUNKS

    def on_space(dz, dx):
        return lax.rem(z + dz + ZS, ZS) * XS + lax.rem(x + dx + XS, XS)

    def in_plane(dy, dx):
        return {"sensor": lax.rem(y + dy, YS) * CORES + core, "space": on_space(0, dx)}

    other_core = y * CORES + (1 - core)
    my_rows = pl.ds(pl.multiple_of(space * rows, rows), rows)

    def piece_of(device, chunk):
        return j_ref.at[:, pl.ds(pl.multiple_of(device * cols + chunk * depth, depth), depth)]

    own = [pltpu.make_async_copy(piece_of(space, c), panel.at[c, my_rows, :], own_sem.at[c]) for c in range(CHUNKS)]
    for copy in own:
        copy.start()
    r_copy = pltpu.make_async_copy(r_ref.at[space], r_own, r_sem)
    r_copy.start()

    barrier = pltpu.get_barrier_semaphore()

    def greet(d, carry):
        pl.semaphore_signal(barrier, inc=1, device_id={"space": lax.rem(space + d, spaces)}, device_id_type=MESH)
        return carry

    lax.fori_loop(1, spaces, greet, 0)
    pl.semaphore_signal(barrier, inc=1, device_id={"sensor": other_core}, device_id_type=MESH)
    for dy in range(1, YS):
        for dx in range(XS):
            pl.semaphore_signal(barrier, inc=1, device_id=in_plane(dy, dx), device_id_type=MESH)
    pl.semaphore_wait(barrier, spaces - 1 + 1 + (YS - 1) * XS)

    for c in range(CHUNKS):

        def start(d, carry, c=c):
            to = on_space(d // XS, lax.rem(d, XS))
            pltpu.make_async_remote_copy(
                src_ref=piece_of(to, c),
                dst_ref=panel.at[c, my_rows, :],
                send_sem=a2a_send.at[c],
                recv_sem=a2a_recv.at[c],
                device_id={"space": to},
                device_id_type=MESH,
            ).start()
            return carry

        lax.fori_loop(1, spaces, start, 0)

    def all_of(c, sem):
        others = panel.at[c, pl.ds(0, params - rows), :]
        pltpu.make_async_copy(others, others, sem).wait()

    tri = blocks * (blocks + 1) // 2
    pack[tri * LANES :, :] = jnp.zeros((pack.shape[0] - tri * LANES, LANES), jnp.float32)
    across = (((1,), (1,)), ((), ()))
    r_copy.wait()
    for c in range(CHUNKS):
        own[c].wait()
        all_of(c, a2a_recv.at[c])
        hi, mid, low = split3(panel[c])
        left = jnp.concatenate([hi, hi, mid, hi, low, mid], axis=1)
        right = jnp.concatenate([hi, mid, hi, low, hi, mid], axis=1)
        at = 0
        for b in range(blocks):
            strip = lax.dot_general(left[b * LANES : (b + 1) * LANES, :], right[b * LANES :, :], across, preferred_element_type=jnp.float32)
            for k in range(blocks - b):
                block = strip[:, k * LANES : (k + 1) * LANES]
                pack[at : at + LANES, :] = block if c == 0 else pack[at : at + LANES, :] + block
                at += LANES
        pieces = depth // LANES
        r_row = jnp.concatenate([r_own[c * pieces + i : c * pieces + i + 1, :] for i in range(pieces)], axis=1)
        rh, rm, rl = split3(jnp.broadcast_to(r_row, (16, depth)))
        r_left = jnp.concatenate([rh, rh, rm, rh, rl, rm], axis=1)
        g = lax.dot_general(r_left, right, across, preferred_element_type=jnp.float32)
        for b in range(blocks):
            pack[at + b : at + b + 1, :] += g[0:1, b * LANES : (b + 1) * LANES]

    half = pack.shape[0] // CORES
    wave = half // WAVES
    strip = wave // YS
    piece = strip // XS
    waves = range(WAVES)

    def remote(src, dst, send, recv, target):
        return pltpu.make_async_remote_copy(src_ref=src, dst_ref=dst, send_sem=send, recv_sem=recv, device_id=target, device_id_type=MESH)

    mine = pl.multiple_of(core * half, half)
    theirs = pl.multiple_of((1 - core) * half, half)

    def strip_of(w, yy, base):
        return pl.ds(pl.multiple_of(base + w * wave + yy * strip, strip), strip)

    def piece_at(w, yy, xx):
        return pl.ds(pl.multiple_of(mine + w * wave + yy * strip + xx * piece, piece), piece)

    def add_up(parts):
        while len(parts) > 1:
            parts = [u + v for u, v in zip(parts[::2], parts[1::2])]
        return parts[0]

    sent = []
    order = (2, 1, 3, 0)
    offsets = [(dy, dx) for dy in order for dx in order if dy or dx]
    core_copies = {}
    for w in waves:
        for dy in order:
            at = strip_of(w, lax.rem(y + dy, YS), theirs)
            core_copies[w, dy] = remote(pack.at[at, :], core_rx.at[w, dy], core_send.at[w, dy], core_recv.at[w, dy], {"sensor": other_core})
            core_copies[w, dy].start()
    sent += core_copies.values()
    plane = {}
    for w in waves:
        for dy in order:
            to_y = lax.rem(y + dy, YS)
            core_copies[w, dy].wait_recv()
            pack[strip_of(w, to_y, mine), :] += core_rx[w, dy]
            for dx in order:
                if dy or dx:
                    k = dy * XS + dx - 1
                    source = pack.at[piece_at(w, to_y, lax.rem(x + dx, XS)), :]
                    plane[w, k] = remote(source, plane_rx.at[w, k], plane_send.at[w, k], plane_recv.at[w, k], in_plane(dy, dx))
                    plane[w, k].start()
    sent += plane.values()
    z_copies = {}
    for w in waves:
        for k in range(YS * XS - 1):
            plane[w, k].wait_recv()
        z_all[w, z] = add_up([pack[piece_at(w, y, x), :]] + [plane_rx[w, k] for k in range(YS * XS - 1)])
        for d in (4, 3, 5, 2, 6, 1, 7):
            z_copies[w, d] = remote(z_all.at[w, z], z_all.at[w, z], z_send.at[w, d - 1], z_recv.at[w, d - 1], {"space": on_space(d, 0)})
            z_copies[w, d].start()
    sent += z_copies.values()
    back = {}
    for w in waves:
        for d in range(1, ZS):
            z_copies[w, d].wait_recv()
        done = out_ref.at[piece_at(w, y, x), :]
        done[...] = add_up([z_all[w, i] for i in range(ZS)])
        for dy, dx in offsets:
            k = dy * XS + dx - 1
            back[w, dy, dx] = remote(done, done, back_send.at[w, k], back_recv.at[w, k], in_plane(dy, dx))
            back[w, dy, dx].start()
    sent += back.values()
    last = []
    for w in waves:
        for dy in (0, 1, 3, 2):
            for dx in order:
                if dy or dx:
                    back[w, dy, dx].wait_recv()
            got = out_ref.at[strip_of(w, lax.rem(y - dy + YS, YS), mine), :]
            last.append(remote(got, got, last_send.at[w, dy], last_recv.at[w, dy], {"sensor": other_core}))
            last[-1].start()
    sent += last
    for copy in last:
        copy.wait_recv()
    for copy in sent:
        copy.wait_send()
    for c in range(CHUNKS):
        all_of(c, a2a_send.at[c])


def normal_matrix(jacobian, residual):
    rows, local = jacobian.shape
    spaces = ZS * XS
    params, cols = rows * spaces, local // spaces
    blocks = params // LANES
    packed = (blocks * (blocks + 1) // 2 + 1) * LANES
    unit = CORES * WAVES * YS * XS * 8
    packed = -(-packed // unit) * unit
    strip = packed // (CORES * WAVES * YS)
    piece = strip // XS
    others = YS * XS - 1
    f32, dma = jnp.float32, pltpu.SemaphoreType.DMA
    return pl.pallas_call(
        regroup_kernel,
        out_shape=pltpu.VMEM((packed, LANES), f32),
        in_specs=[pl.BlockSpec(memory_space=pl.ANY), pl.BlockSpec(memory_space=pl.ANY)],
        out_specs=pl.BlockSpec(memory_space=pltpu.VMEM),
        scratch_shapes=[
            pltpu.VMEM((CHUNKS, params, cols // CHUNKS), f32),
            pltpu.VMEM((cols // LANES, LANES), f32),
            pltpu.VMEM((packed, LANES), f32),
            pltpu.VMEM((WAVES, YS, strip, LANES), f32),
            pltpu.VMEM((WAVES, others, piece, LANES), f32),
            pltpu.VMEM((WAVES, ZS, piece, LANES), f32),
            dma((CHUNKS,)), dma,
            dma((CHUNKS,)), dma((CHUNKS,)),
            dma((WAVES, YS)), dma((WAVES, YS)),
            dma((WAVES, others)), dma((WAVES, others)),
            dma((WAVES, ZS - 1)), dma((WAVES, ZS - 1)),
            dma((WAVES, others)), dma((WAVES, others)),
            dma((WAVES, YS)), dma((WAVES, YS)),
        ],
        compiler_params=pltpu.CompilerParams(collective_id=0, has_side_effects=True, vmem_limit_bytes=56 << 20),
    )(jacobian, residual.reshape(spaces, -1, LANES))


def block_at(b, c, blocks):
    return b * blocks - b * (b - 1) // 2 + (c - b)


def solve_kernel(blocks, packed, damping, x_ref, mat):
    tri = blocks * (blocks + 1) // 2
    wide = blocks + 1
    eye = lax.broadcasted_iota(jnp.int32, (LANES, LANES), 0) == lax.broadcasted_iota(jnp.int32, (LANES, LANES), 1)
    lam = damping[0]
    scale_rows, scale_cols = [], []
    for b in range(blocks):
        at = block_at(b, b, blocks) * LANES
        diag = jnp.where(eye, packed[at : at + LANES, :], 0.0)
        scale_rows.append(lax.rsqrt(jnp.sum(diag, axis=0, keepdims=True)))
        scale_cols.append(lax.rsqrt(jnp.sum(diag, axis=1, keepdims=True)))
    for b in range(blocks):
        for c in range(b, blocks):
            at = block_at(b, c, blocks) * LANES
            v = packed[at : at + LANES, :] * scale_cols[b] * scale_rows[c]
            if b == c:
                v = jnp.where(eye, 1.0 + lam, v)
            mat[b * LANES : (b + 1) * LANES, c * LANES : (c + 1) * LANES] = v
        g_row = packed[tri * LANES + b : tri * LANES + b + 1, :] * scale_rows[b]
        g_col = jnp.sum(jnp.where(eye, g_row, 0.0), axis=1, keepdims=True)
        mat[b * LANES : (b + 1) * LANES, blocks * LANES :] = jnp.broadcast_to(g_col, (LANES, LANES))

    lane = lax.broadcasted_iota(jnp.int32, (8, LANES), 1)
    sub = lax.broadcasted_iota(jnp.int32, (8, LANES), 0)

    def row(v, i):
        return jnp.broadcast_to(v[i : i + 1, :], (8, LANES))

    def invert(t, own):
        wide_by = PANEL // 8
        for h in range(SLAB // PANEL):
            mine = range(h * wide_by, (h + 1) * wide_by)
            first = own + h * PANEL

            def column(v, q):
                return jnp.broadcast_to(v[:, first + q : first + q + 1], (8, LANES))

            cols = [[column(t[i], q) for i in mine] for q in range(PANEL)]
            rows_of = [t[i] for i in mine]
            for p in range(0, PANEL, 2):
                g, k = divmod(p, 8)
                at, bt, ct = row(cols[p][g], k), row(cols[p + 1][g], k), row(cols[p + 1][g], k + 1)
                r = pltpu.reciprocal(at * ct - bt * bt, approx=True)
                if p == 0:
                    tie = r * 0.0
                av, bv, cv = at * r, bt * r, ct * r
                left, right = list(cols[p]), list(cols[p + 1])
                left[g] = left[g] - jnp.where(sub == k, 1.0, 0.0)
                right[g] = right[g] - jnp.where(sub == k + 1, 1.0, 0.0)
                by0 = [x * cv - y * bv for x, y in zip(left, right)]
                by1 = [y * av - x * bv for x, y in zip(left, right)]

                def eliminate(z):
                    z0, z1 = row(z[g], k), row(z[g], k + 1)
                    return [v - (x * z0 + y * z1) for v, x, y in zip(z, by0, by1)]

                for q in range(p + 2, PANEL):
                    cols[q] = eliminate(cols[q])
                rows_of = eliminate(rows_of)
            u_rows = [row(rows_of[q // 8], q % 8) for q in range(PANEL)]
            others = {i: t[i] + tie for i in range(SLAB // 8) if i not in mine}
            parts = {i: [] for i in others}
            for q in range(PANEL):
                for i in others:
                    parts[i].append(column(others[i], q) * u_rows[q])
            new = []
            for i in range(SLAB // 8):
                if i in mine:
                    new.append(rows_of[i - mine[0]])
                    continue
                while len(parts[i]) > 1:
                    parts[i] = [x + y for x, y in zip(parts[i][::2], parts[i][1::2])]
                new.append(t[i] - parts[i][0])
            t = new
        return t

    def slab_step(b, inner):
        top = b * LANES + inner * SLAB
        own = inner * SLAB
        rest = LANES - SLAB - own
        s = mat[top : top + SLAB, b * LANES :]
        t = []
        for i in range(SLAB // 8):
            unit = jnp.where(lane == sub + (rest + 8 * i), 1.0, 0.0)
            t.append(jnp.where((lane >= own) & (lane < own + SLAB), s[8 * i : 8 * i + 8, :LANES], unit))
        inv = jnp.concatenate(invert(t, own), axis=0)
        skip = LANES if inner else 0
        sh, sm, sl = split3(s[:, skip:])
        ih, im, il = split3(inv)
        weights = jnp.concatenate([ih, ih, im, ih, il, im], axis=0)
        stack = jnp.concatenate([sh, sm, sh, sl, sh, sm], axis=0)
        over = (((0,), (0,)), ((), ()))
        u = lax.dot_general(weights, stack, over, preferred_element_type=jnp.float32)[rest : rest + SLAB, :]
        mat[top : top + SLAB, b * LANES + skip :] = u
        count = (blocks - b) * LANES - skip
        if count == 0:
            return

        def later(v):
            v = v[:, :count]
            if inner:
                return v
            edge = jnp.where(lax.broadcasted_iota(jnp.int32, (SLAB, LANES), 1) >= SLAB, v[:, :LANES], jnp.zeros((SLAB, LANES), v.dtype))
            return edge if count == LANES else jnp.concatenate([edge, v[:, LANES:]], axis=1)

        xh, xm, xl = later(sh), later(sm), later(sl)
        uh, um, ul = split3(u)
        left = jnp.concatenate([xh, xh, xm, xh, xl, xm], axis=0)
        right = jnp.concatenate([uh, um, uh, ul, uh, um], axis=0)
        for o in range(0, count, LANES):
            at = b * LANES + skip + o
            prod = lax.dot_general(left[:, o : o + LANES], right[:, o:], over, preferred_element_type=jnp.float32)
            mat[at : at + LANES, at:] -= prod

    for b in range(blocks):
        for inner in range(LANES // SLAB):
            slab_step(b, inner)

    per = LANES // SLAB
    xs = [jnp.zeros((1, LANES), jnp.float32) for _ in range(blocks)]
    for k in reversed(range(blocks * per)):
        b, inner = divmod(k, per)
        u = mat[k * SLAB : (k + 1) * SLAB, :]
        acc = None
        for t in range(b + (inner == per - 1), blocks):
            term = u[:, t * LANES : (t + 1) * LANES] * xs[t]
            acc = term if acc is None else acc + term
        col = u[:, blocks * LANES :]
        if acc is not None:
            col = col - jnp.sum(acc, axis=1, keepdims=True)
        pick = lax.broadcasted_iota(jnp.int32, (SLAB, LANES), 1) == lax.broadcasted_iota(jnp.int32, (SLAB, LANES), 0) + inner * SLAB
        xs[b] = xs[b] + jnp.sum(jnp.where(pick, col, 0.0), axis=0, keepdims=True)
    for b in range(blocks):
        x_ref[b : b + 1, :] = -(xs[b] * scale_rows[b])


def solve(packed, damping, params):
    blocks = params // LANES
    out = pl.pallas_call(
        functools.partial(solve_kernel, blocks),
        out_shape=jax.ShapeDtypeStruct((blocks, LANES), jnp.float32),
        in_specs=[pl.BlockSpec(memory_space=pltpu.VMEM), pl.BlockSpec(memory_space=pltpu.SMEM)],
        out_specs=pl.BlockSpec(memory_space=pltpu.VMEM),
        scratch_shapes=[pltpu.VMEM((params, params + LANES), jnp.float32)],
        compiler_params=pltpu.CompilerParams(vmem_limit_bytes=24 << 20),
    )(packed, damping)
    return out.reshape(params)


def per_device(jacobian, residual, damping):
    params = jacobian.shape[0] * ZS * XS
    return solve(normal_matrix(jacobian, residual), damping, params)


def solution(mesh):
    placed = (P("space", "sensor"), P("sensor"), P())
    return jax.shard_map(per_device, mesh=mesh, in_specs=placed, out_specs=P(), check_vma=False)
```

```python
import functools
import jax
import jax.numpy as jnp
from jax import lax
from jax.experimental import pallas as pl
from jax.experimental.pallas import tpu as pltpu
from jax.sharding import PartitionSpec as P

LANES = 128
MESH = pl.DeviceIdType.MESH
YS, CORES, ZS, XS = 4, 2, 8, 4
CHUNKS = 4
SLAB = 64
PANEL = 16


def split3(v):
    hi = v.astype(jnp.bfloat16)
    rest = v - hi.astype(jnp.float32)
    mid = rest.astype(jnp.bfloat16)
    low = (rest - mid.astype(jnp.float32)).astype(jnp.bfloat16)
    return hi, mid, low


def block_at(b, c, blocks):
    return b * blocks - b * (b - 1) // 2 + (c - b)


def wave_pieces(packed):
    total = packed // (CORES * YS * XS)
    first = -(-total // 16) * 8
    return first, total - first


def regroup_kernel(j_ref, r_ref, out_ref, panel, r_own, pack, core_rx, plane_rx, z_all, own_sem, r_sem,
                   a2a_send, a2a_recv, core_send, core_recv, plane_send, plane_recv, z_send, z_recv,
                   back_send, back_recv, last_send, last_recv):
    sensor, space = lax.axis_index("sensor"), lax.axis_index("space")
    y, core = sensor // CORES, sensor % CORES
    z, x = space // XS, space % XS
    spaces = ZS * XS
    rows = j_ref.shape[0]
    cols = j_ref.shape[1] // spaces
    params = rows * spaces
    blocks = params // LANES
    depth = cols // CHUNKS

    def on_space(dz, dx):
        return lax.rem(z + dz + ZS, ZS) * XS + lax.rem(x + dx + XS, XS)

    def in_plane(dy, dx):
        return {"sensor": lax.rem(y + dy, YS) * CORES + core, "space": on_space(0, dx)}

    other_core = y * CORES + (1 - core)
    my_rows = pl.ds(pl.multiple_of(space * rows, rows), rows)

    def piece_of(device, chunk):
        return j_ref.at[:, pl.ds(pl.multiple_of(device * cols + chunk * depth, depth), depth)]

    own = [pltpu.make_async_copy(piece_of(space, c), panel.at[c, my_rows, :], own_sem.at[c]) for c in range(CHUNKS)]
    for copy in own:
        copy.start()
    r_copy = pltpu.make_async_copy(r_ref.at[space], r_own, r_sem)
    r_copy.start()

    barrier = pltpu.get_barrier_semaphore()

    def greet(d, carry):
        pl.semaphore_signal(barrier, inc=1, device_id={"space": lax.rem(space + d, spaces)}, device_id_type=MESH)
        return carry

    lax.fori_loop(1, spaces, greet, 0)
    pl.semaphore_signal(barrier, inc=1, device_id={"sensor": other_core}, device_id_type=MESH)
    for dy in range(1, YS):
        for dx in range(XS):
            pl.semaphore_signal(barrier, inc=1, device_id=in_plane(dy, dx), device_id_type=MESH)
    pl.semaphore_wait(barrier, spaces - 1 + 1 + (YS - 1) * XS)

    for c in range(CHUNKS):

        def start(d, carry, c=c):
            to = on_space(d // XS, lax.rem(d, XS))
            pltpu.make_async_remote_copy(
                src_ref=piece_of(to, c),
                dst_ref=panel.at[c, my_rows, :],
                send_sem=a2a_send.at[c],
                recv_sem=a2a_recv.at[c],
                device_id={"space": to},
                device_id_type=MESH,
            ).start()
            return carry

        lax.fori_loop(1, spaces, start, 0)

    def all_of(c, sem):
        others = panel.at[c, pl.ds(0, params - rows), :]
        pltpu.make_async_copy(others, others, sem).wait()

    across = (((1,), (1,)), ((), ()))
    r_copy.wait()
    for c in range(CHUNKS):
        own[c].wait()
        all_of(c, a2a_recv.at[c])
        hi, mid, low = split3(panel[c])
        left = jnp.concatenate([hi, hi, mid, hi, low, mid], axis=1)
        right = jnp.concatenate([hi, mid, hi, low, hi, mid], axis=1)
        at = 0
        for b in range(blocks):
            strip = lax.dot_general(left[b * LANES : (b + 1) * LANES, :], right[b * LANES :, :], across, preferred_element_type=jnp.float32)
            for k in range(blocks - b):
                block = strip[:, k * LANES : (k + 1) * LANES]
                pack[at : at + LANES, :] = block if c == 0 else pack[at : at + LANES, :] + block
                at += LANES
        pieces = depth // LANES
        r_row = jnp.concatenate([r_own[c * pieces + i : c * pieces + i + 1, :] for i in range(pieces)], axis=1)
        rh, rm, rl = split3(jnp.broadcast_to(r_row, (16, depth)))
        r_left = jnp.concatenate([rh, rh, rm, rh, rl, rm], axis=1)
        g = lax.dot_general(r_left, right, across, preferred_element_type=jnp.float32)
        g_row = g[0:1, :] if c == 0 else g_row + g[0:1, :]
    lane = lax.broadcasted_iota(jnp.int32, (1, LANES), 1)
    for b in range(blocks):
        end = (block_at(b, b, blocks) + 1) * LANES
        part = g_row[:, b * LANES : (b + 1) * LANES]
        pack[end - 1 : end, :] = jnp.where(lane < LANES - 1, part, pack[end - 1 : end, :])
        pack[end - 2 : end - 1, :] = jnp.where(lane == 0, part[:, LANES - 1 :], pack[end - 2 : end - 1, :])

    half = pack.shape[0] // CORES
    pieces = wave_pieces(pack.shape[0])
    waves = range(len(pieces))
    starts = [sum(pieces[:w]) * YS * XS for w in waves]

    def remote(src, dst, send, recv, target):
        return pltpu.make_async_remote_copy(src_ref=src, dst_ref=dst, send_sem=send, recv_sem=recv, device_id=target, device_id_type=MESH)

    mine = pl.multiple_of(core * half, half)
    theirs = pl.multiple_of((1 - core) * half, half)

    def strip_of(w, yy, base):
        strip = pieces[w] * XS
        return pl.ds(pl.multiple_of(base + starts[w] + yy * strip, 8), strip)

    def piece_at(w, yy, xx):
        return pl.ds(pl.multiple_of(mine + starts[w] + (yy * XS + xx) * pieces[w], 8), pieces[w])

    def add_up(parts):
        while len(parts) > 1:
            parts = [u + v for u, v in zip(parts[::2], parts[1::2])]
        return parts[0]

    def wait_for(region, sem):
        pltpu.make_async_copy(region, region, sem).wait()

    order = (2, 1, 3, 0)
    offsets = [(dy, dx) for dy in order for dx in order if dy or dx]
    core_copies = {}
    for w in waves:
        for dy in order:
            at = strip_of(w, lax.rem(y + dy, YS), theirs)
            core_copies[w, dy] = remote(pack.at[at, :], core_rx.at[w, dy, pl.ds(0, pieces[w] * XS), :], core_send, core_recv.at[w, dy], {"sensor": other_core})
            core_copies[w, dy].start()
    for w in waves:
        for dy in order:
            to_y = lax.rem(y + dy, YS)
            core_copies[w, dy].wait_recv()
            pack[strip_of(w, to_y, mine), :] += core_rx[w, dy, : pieces[w] * XS, :]
            for dx in order:
                if dy or dx:
                    source = pack.at[piece_at(w, to_y, lax.rem(x + dx, XS)), :]
                    landing = plane_rx.at[w, dy * XS + dx - 1, pl.ds(0, pieces[w]), :]
                    remote(source, landing, plane_send.at[w], plane_recv.at[w], in_plane(dy, dx)).start()
    for w in waves:
        wait_for(plane_rx.at[w, :, pl.ds(0, pieces[w]), :], plane_recv.at[w])
        z_all[w, z, : pieces[w], :] = add_up([pack[piece_at(w, y, x), :]] + [plane_rx[w, k, : pieces[w], :] for k in range(YS * XS - 1)])
        for d in (4, 3, 5, 2, 6, 1, 7):
            own_slot = z_all.at[w, z, pl.ds(0, pieces[w]), :]
            remote(own_slot, own_slot, z_send.at[w], z_recv.at[w], {"space": on_space(d, 0)}).start()
    for w in waves:
        wait_for(z_all.at[w, pl.ds(0, ZS - 1), pl.ds(0, pieces[w]), :], z_recv.at[w])
        done = out_ref.at[piece_at(w, y, x), :]
        done[...] = add_up([z_all[w, i, : pieces[w], :] for i in range(ZS)])
        for dy, dx in offsets:
            remote(done, done, back_send.at[w], back_recv.at[w, dy], in_plane(dy, dx)).start()
    for w in waves:
        for dy in (0, 1, 3, 2):
            wait_for(plane_rx.at[w, pl.ds(0, XS if dy else XS - 1), pl.ds(0, pieces[w]), :], back_recv.at[w, dy])
            got = out_ref.at[strip_of(w, lax.rem(y - dy + YS, YS), mine), :]
            remote(got, got, last_send, last_recv, {"sensor": other_core}).start()
    my_half, other_half = out_ref.at[pl.ds(mine, half), :], out_ref.at[pl.ds(theirs, half), :]
    wait_for(other_half, last_recv)
    wait_for(my_half, last_send)
    wait_for(my_half, core_send)
    for w in waves:
        wait_for(plane_rx.at[w, :, pl.ds(0, pieces[w]), :], plane_send.at[w])
        wait_for(z_all.at[w, pl.ds(0, ZS - 1), pl.ds(0, pieces[w]), :], z_send.at[w])
        wait_for(plane_rx.at[w, :, pl.ds(0, pieces[w]), :], back_send.at[w])
    for c in range(CHUNKS):
        all_of(c, a2a_send.at[c])


def normal_matrix(jacobian, residual):
    rows, local = jacobian.shape
    spaces = ZS * XS
    params, cols = rows * spaces, local // spaces
    blocks = params // LANES
    packed = blocks * (blocks + 1) // 2 * LANES
    piece = max(wave_pieces(packed))
    strip = piece * XS
    waves = len(wave_pieces(packed))
    others = YS * XS - 1
    f32, dma = jnp.float32, pltpu.SemaphoreType.DMA
    return pl.pallas_call(
        regroup_kernel,
        out_shape=pltpu.VMEM((packed, LANES), f32),
        in_specs=[pl.BlockSpec(memory_space=pl.ANY), pl.BlockSpec(memory_space=pl.ANY)],
        out_specs=pl.BlockSpec(memory_space=pltpu.VMEM),
        scratch_shapes=[
            pltpu.VMEM((CHUNKS, params, cols // CHUNKS), f32),
            pltpu.VMEM((cols // LANES, LANES), f32),
            pltpu.VMEM((packed, LANES), f32),
            pltpu.VMEM((waves, YS, strip, LANES), f32),
            pltpu.VMEM((waves, others, piece, LANES), f32),
            pltpu.VMEM((waves, ZS, piece, LANES), f32),
            dma((CHUNKS,)), dma,
            dma((CHUNKS,)), dma((CHUNKS,)),
            dma, dma((waves, YS)),
            dma((waves,)), dma((waves,)),
            dma((waves,)), dma((waves,)),
            dma((waves,)), dma((waves, YS)),
            dma, dma,
        ],
        compiler_params=pltpu.CompilerParams(collective_id=0, has_side_effects=True, vmem_limit_bytes=56 << 20),
    )(jacobian, residual.reshape(spaces, -1, LANES))


def solve_kernel(blocks, packed, damping, x_ref, mat):
    wide = blocks + 1
    deep = lax.broadcasted_iota(jnp.int32, (LANES, LANES), 0)
    across = lax.broadcasted_iota(jnp.int32, (LANES, LANES), 1)
    wide_lane = lax.broadcasted_iota(jnp.int32, (1, LANES), 1)
    eye = deep == across
    lam = damping[0]
    scale_rows, scale_cols = [], []
    for b in range(blocks):
        at = block_at(b, b, blocks) * LANES
        diag = jnp.where(eye, packed[at : at + LANES, :], 0.0)
        scale_rows.append(lax.rsqrt(jnp.sum(diag, axis=0, keepdims=True)))
        scale_cols.append(lax.rsqrt(jnp.sum(diag, axis=1, keepdims=True)))
    for b in range(blocks):
        for c in range(b, blocks):
            at = block_at(b, c, blocks) * LANES
            v = packed[at : at + LANES, :]
            if b == c:
                g_row = jnp.where(wide_lane < LANES - 1, v[LANES - 1 :, :], v[LANES - 2 : LANES - 1, 0:1])
                last = jnp.sum(jnp.where(eye, v[:, LANES - 1 :], 0.0), axis=0, keepdims=True)
                v = jnp.where(deep == LANES - 1, last, v)
                v = jnp.where((deep == LANES - 2) & (across == 0), v[0:1, LANES - 2 : LANES - 1], v)
            v = v * scale_cols[b] * scale_rows[c]
            if b == c:
                v = jnp.where(eye, 1.0 + lam, v)
            mat[b * LANES : (b + 1) * LANES, c * LANES : (c + 1) * LANES] = v
            if b == c:
                g_col = jnp.sum(jnp.where(eye, g_row * scale_rows[b], 0.0), axis=1, keepdims=True)
        mat[b * LANES : (b + 1) * LANES, blocks * LANES :] = jnp.broadcast_to(g_col, (LANES, LANES))

    lane = lax.broadcasted_iota(jnp.int32, (8, LANES), 1)
    sub = lax.broadcasted_iota(jnp.int32, (8, LANES), 0)

    def row(v, i):
        return jnp.broadcast_to(v[i : i + 1, :], (8, LANES))

    def invert(t, own):
        wide_by = PANEL // 8
        for h in range(SLAB // PANEL):
            mine = range(h * wide_by, (h + 1) * wide_by)
            first = own + h * PANEL

            def column(v, q):
                return jnp.broadcast_to(v[:, first + q : first + q + 1], (8, LANES))

            cols = [[column(t[i], q) for i in mine] for q in range(PANEL)]
            rows_of = [t[i] for i in mine]
            for p in range(0, PANEL, 2):
                g, k = divmod(p, 8)
                at, bt, ct = row(cols[p][g], k), row(cols[p + 1][g], k), row(cols[p + 1][g], k + 1)
                r = pltpu.reciprocal(at * ct - bt * bt, approx=True)
                if p == 0:
                    tie = r * 0.0
                av, bv, cv = at * r, bt * r, ct * r
                left, right = list(cols[p]), list(cols[p + 1])
                left[g] = left[g] - jnp.where(sub == k, 1.0, 0.0)
                right[g] = right[g] - jnp.where(sub == k + 1, 1.0, 0.0)
                by0 = [x * cv - y * bv for x, y in zip(left, right)]
                by1 = [y * av - x * bv for x, y in zip(left, right)]

                def eliminate(z):
                    z0, z1 = row(z[g], k), row(z[g], k + 1)
                    return [v - (x * z0 + y * z1) for v, x, y in zip(z, by0, by1)]

                for q in range(p + 2, PANEL):
                    cols[q] = eliminate(cols[q])
                rows_of = eliminate(rows_of)
            u_rows = [row(rows_of[q // 8], q % 8) for q in range(PANEL)]
            others = {i: t[i] + tie for i in range(SLAB // 8) if i not in mine}
            parts = {i: [] for i in others}
            for q in range(PANEL):
                for i in others:
                    parts[i].append(column(others[i], q) * u_rows[q])
            new = []
            for i in range(SLAB // 8):
                if i in mine:
                    new.append(rows_of[i - mine[0]])
                    continue
                while len(parts[i]) > 1:
                    parts[i] = [x + y for x, y in zip(parts[i][::2], parts[i][1::2])]
                new.append(t[i] - parts[i][0])
            t = new
        return t

    def slab_step(b, inner):
        top = b * LANES + inner * SLAB
        own = inner * SLAB
        rest = LANES - SLAB - own
        s = mat[top : top + SLAB, b * LANES :]
        t = []
        for i in range(SLAB // 8):
            unit = jnp.where(lane == sub + (rest + 8 * i), 1.0, 0.0)
            t.append(jnp.where((lane >= own) & (lane < own + SLAB), s[8 * i : 8 * i + 8, :LANES], unit))
        inv = jnp.concatenate(invert(t, own), axis=0)
        skip = LANES if inner else 0
        sh, sm, sl = split3(s[:, skip:])
        ih, im, il = split3(inv)
        weights = jnp.concatenate([ih, ih, im, ih, il, im], axis=0)
        stack = jnp.concatenate([sh, sm, sh, sl, sh, sm], axis=0)
        over = (((0,), (0,)), ((), ()))
        u = lax.dot_general(weights, stack, over, preferred_element_type=jnp.float32)[rest : rest + SLAB, :]
        mat[top : top + SLAB, b * LANES + skip :] = u
        count = (blocks - b) * LANES - skip
        if count == 0:
            return

        def later(v):
            v = v[:, :count]
            if inner:
                return v
            edge = jnp.where(lax.broadcasted_iota(jnp.int32, (SLAB, LANES), 1) >= SLAB, v[:, :LANES], jnp.zeros((SLAB, LANES), v.dtype))
            return edge if count == LANES else jnp.concatenate([edge, v[:, LANES:]], axis=1)

        xh, xm, xl = later(sh), later(sm), later(sl)
        uh, um, ul = split3(u)
        left = jnp.concatenate([xh, xh, xm, xh, xl, xm], axis=0)
        right = jnp.concatenate([uh, um, uh, ul, uh, um], axis=0)
        for o in range(0, count, LANES):
            at = b * LANES + skip + o
            prod = lax.dot_general(left[:, o : o + LANES], right[:, o:], over, preferred_element_type=jnp.float32)
            mat[at : at + LANES, at:] -= prod

    for b in range(blocks):
        for inner in range(LANES // SLAB):
            slab_step(b, inner)

    per = LANES // SLAB
    xs = [jnp.zeros((1, LANES), jnp.float32) for _ in range(blocks)]
    for k in reversed(range(blocks * per)):
        b, inner = divmod(k, per)
        u = mat[k * SLAB : (k + 1) * SLAB, :]
        acc = None
        for t in range(b + (inner == per - 1), blocks):
            term = u[:, t * LANES : (t + 1) * LANES] * xs[t]
            acc = term if acc is None else acc + term
        col = u[:, blocks * LANES :]
        if acc is not None:
            col = col - jnp.sum(acc, axis=1, keepdims=True)
        pick = lax.broadcasted_iota(jnp.int32, (SLAB, LANES), 1) == lax.broadcasted_iota(jnp.int32, (SLAB, LANES), 0) + inner * SLAB
        xs[b] = xs[b] + jnp.sum(jnp.where(pick, col, 0.0), axis=0, keepdims=True)
    for b in range(blocks):
        x_ref[b : b + 1, :] = -(xs[b] * scale_rows[b])


def solve(packed, damping, params):
    blocks = params // LANES
    out = pl.pallas_call(
        functools.partial(solve_kernel, blocks),
        out_shape=jax.ShapeDtypeStruct((blocks, LANES), jnp.float32),
        in_specs=[pl.BlockSpec(memory_space=pltpu.VMEM), pl.BlockSpec(memory_space=pltpu.SMEM)],
        out_specs=pl.BlockSpec(memory_space=pltpu.VMEM),
        scratch_shapes=[pltpu.VMEM((params, params + LANES), jnp.float32)],
        compiler_params=pltpu.CompilerParams(vmem_limit_bytes=24 << 20),
    )(packed, damping)
    return out.reshape(params)


def per_device(jacobian, residual, damping):
    params = jacobian.shape[0] * ZS * XS
    return solve(normal_matrix(jacobian, residual), damping, params)


def solution(mesh):
    placed = (P("space", "sensor"), P("sensor"), P())
    return jax.shard_map(per_device, mesh=mesh, in_specs=placed, out_specs=P(), check_vma=False)
```

```python
import functools
import jax
import jax.numpy as jnp
from jax import lax
from jax.experimental import pallas as pl
from jax.experimental.pallas import tpu as pltpu
from jax.sharding import PartitionSpec as P

LANES = 128
MESH = pl.DeviceIdType.MESH
YS, CORES, ZS, XS = 4, 2, 8, 4
CHUNKS = 4
SLAB = 64
PANEL = 16


def split3(v):
    hi = v.astype(jnp.bfloat16)
    rest = v - hi.astype(jnp.float32)
    mid = rest.astype(jnp.bfloat16)
    low = (rest - mid.astype(jnp.float32)).astype(jnp.bfloat16)
    return hi, mid, low


def block_at(b, c, blocks):
    return b * blocks - b * (b - 1) // 2 + (c - b)


def wave_pieces(packed):
    total = packed // (CORES * YS * XS)
    first = total // 16 * 8
    return first, total - first


def regroup_kernel(j_ref, r_ref, out_ref, panel, r_own, pack, core_rx, plane_rx, z_all, own_sem, r_sem,
                   a2a_send, a2a_recv, core_send, core_recv, plane_send, plane_recv, z_send, z_recv,
                   back_send, back_recv, last_send, last_recv):
    sensor, space = lax.axis_index("sensor"), lax.axis_index("space")
    y, core = sensor // CORES, sensor % CORES
    z, x = space // XS, space % XS
    spaces = ZS * XS
    rows = j_ref.shape[0]
    cols = j_ref.shape[1] // spaces
    params = rows * spaces
    blocks = params // LANES
    depth = cols // CHUNKS

    def on_space(dz, dx):
        return lax.rem(z + dz + ZS, ZS) * XS + lax.rem(x + dx + XS, XS)

    def in_plane(dy, dx):
        return {"sensor": lax.rem(y + dy, YS) * CORES + core, "space": on_space(0, dx)}

    other_core = y * CORES + (1 - core)
    my_rows = pl.ds(pl.multiple_of(space * rows, rows), rows)

    def piece_of(device, chunk):
        return j_ref.at[:, pl.ds(pl.multiple_of(device * cols + chunk * depth, depth), depth)]

    own = [pltpu.make_async_copy(piece_of(space, c), panel.at[c, my_rows, :], own_sem.at[c]) for c in range(CHUNKS)]
    for copy in own:
        copy.start()
    r_copy = pltpu.make_async_copy(r_ref.at[space], r_own, r_sem)
    r_copy.start()

    barrier = pltpu.get_barrier_semaphore()

    def greet(d, carry):
        pl.semaphore_signal(barrier, inc=1, device_id={"space": lax.rem(space + d, spaces)}, device_id_type=MESH)
        return carry

    lax.fori_loop(1, spaces, greet, 0)
    pl.semaphore_signal(barrier, inc=1, device_id={"sensor": other_core}, device_id_type=MESH)
    for dy in range(1, YS):
        for dx in range(XS):
            pl.semaphore_signal(barrier, inc=1, device_id=in_plane(dy, dx), device_id_type=MESH)
    pl.semaphore_wait(barrier, spaces - 1 + 1 + (YS - 1) * XS)

    for c in range(CHUNKS):

        def start(d, carry, c=c):
            to = on_space(d // XS, lax.rem(d, XS))
            pltpu.make_async_remote_copy(
                src_ref=piece_of(to, c),
                dst_ref=panel.at[c, my_rows, :],
                send_sem=a2a_send.at[c],
                recv_sem=a2a_recv.at[c],
                device_id={"space": to},
                device_id_type=MESH,
            ).start()
            return carry

        lax.fori_loop(1, spaces, start, 0)

    def all_of(c, sem):
        others = panel.at[c, pl.ds(0, params - rows), :]
        pltpu.make_async_copy(others, others, sem).wait()

    half = pack.shape[0] // CORES
    pieces = wave_pieces(pack.shape[0])
    waves = range(len(pieces))
    starts = [sum(pieces[:w]) * YS * XS for w in waves]

    def remote(src, dst, send, recv, target):
        return pltpu.make_async_remote_copy(src_ref=src, dst_ref=dst, send_sem=send, recv_sem=recv, device_id=target, device_id_type=MESH)

    mine = pl.multiple_of(core * half, half)
    theirs = pl.multiple_of((1 - core) * half, half)

    def strip_of(w, yy, base):
        strip = pieces[w] * XS
        return pl.ds(pl.multiple_of(base + starts[w] + yy * strip, 8), strip)

    def piece_at(w, yy, xx):
        return pl.ds(pl.multiple_of(mine + starts[w] + (yy * XS + xx) * pieces[w], 8), pieces[w])

    def add_up(parts):
        while len(parts) > 1:
            parts = [u + v for u, v in zip(parts[::2], parts[1::2])]
        return parts[0]

    order = (2, 1, 3, 0)
    core_copies = {}
    for w in waves:
        for dy in order:
            at = strip_of(w, lax.rem(y + dy, YS), theirs)
            core_copies[w, dy] = remote(pack.at[at, :], core_rx.at[w, dy, pl.ds(0, pieces[w] * XS), :], core_send, core_recv.at[w, dy], {"sensor": other_core})

    across = (((1,), (1,)), ((), ()))
    lane = lax.broadcasted_iota(jnp.int32, (1, LANES), 1)
    every = [(b, k) for b in range(blocks) for k in range(b, blocks)]
    share = len(every) // CORES

    def gram_part(part, left, right, first, g_row):
        chosen = every[part * share : (part + 1) * share]
        for b in range(blocks):
            ks = [k for i, k in chosen if i == b]
            if not ks:
                continue
            term = lax.dot_general(
                left[b * LANES : (b + 1) * LANES, :],
                right[ks[0] * LANES : (ks[-1] + 1) * LANES, :],
                across,
                preferred_element_type=jnp.float32,
            )
            for i, k in enumerate(ks):
                at = block_at(b, k, blocks) * LANES
                block = term[:, i * LANES : (i + 1) * LANES]
                pack[at : at + LANES, :] = block if first else pack[at : at + LANES, :] + block
            if g_row is not None and b in ks:
                end = (block_at(b, b, blocks) + 1) * LANES
                g = g_row[:, b * LANES : (b + 1) * LANES]
                pack[end - 1 : end, :] = jnp.where(lane < LANES - 1, g, pack[end - 1 : end, :])
                pack[end - 2 : end - 1, :] = jnp.where(lane == 0, g[:, LANES - 1 :], pack[end - 2 : end - 1, :])

    r_copy.wait()
    for c in range(CHUNKS):
        own[c].wait()
        all_of(c, a2a_recv.at[c])
        hi, mid, low = split3(panel[c])
        left = jnp.concatenate([hi, hi, mid, hi, low, mid], axis=1)
        right = jnp.concatenate([hi, mid, hi, low, hi, mid], axis=1)
        span = depth // LANES
        r_row = jnp.concatenate([r_own[c * span + i : c * span + i + 1, :] for i in range(span)], axis=1)
        rh, rm, rl = split3(jnp.broadcast_to(r_row, (16, depth)))
        r_left = jnp.concatenate([rh, rh, rm, rh, rl, rm], axis=1)
        g = lax.dot_general(r_left, right, across, preferred_element_type=jnp.float32)
        g_row = g[0:1, :] if c == 0 else g_row + g[0:1, :]
        if c < CHUNKS - 1:
            for part in range(CORES):
                gram_part(part, left, right, c == 0, None)
            continue
        for me in range(CORES):

            @pl.when(core == me)
            def _(me=me):
                gram_part(1 - me, left, right, CHUNKS == 1, g_row)
                for copy in core_copies.values():
                    copy.start()
                gram_part(me, left, right, CHUNKS == 1, g_row)

    def wait_for(region, sem):
        pltpu.make_async_copy(region, region, sem).wait()

    offsets = [(dy, dx) for dy in order for dx in order if dy or dx]
    for w in waves:
        for dy in order:
            to_y = lax.rem(y + dy, YS)
            core_copies[w, dy].wait_recv()
            pack[strip_of(w, to_y, mine), :] += core_rx[w, dy, : pieces[w] * XS, :]
            for dx in order:
                if dy or dx:
                    source = pack.at[piece_at(w, to_y, lax.rem(x + dx, XS)), :]
                    landing = plane_rx.at[w, dy * XS + dx - 1, pl.ds(0, pieces[w]), :]
                    remote(source, landing, plane_send.at[w], plane_recv.at[w], in_plane(dy, dx)).start()
    for w in waves:
        wait_for(plane_rx.at[w, :, pl.ds(0, pieces[w]), :], plane_recv.at[w])
        z_all[w, z, : pieces[w], :] = add_up([pack[piece_at(w, y, x), :]] + [plane_rx[w, k, : pieces[w], :] for k in range(YS * XS - 1)])
        for d in (4, 3, 5, 2, 6, 1, 7):
            own_slot = z_all.at[w, z, pl.ds(0, pieces[w]), :]
            remote(own_slot, own_slot, z_send.at[w], z_recv.at[w], {"space": on_space(d, 0)}).start()
    for w in waves:
        wait_for(z_all.at[w, pl.ds(0, ZS - 1), pl.ds(0, pieces[w]), :], z_recv.at[w])
        done = out_ref.at[piece_at(w, y, x), :]
        done[...] = add_up([z_all[w, i, : pieces[w], :] for i in range(ZS)])
        for dy, dx in offsets:
            remote(done, done, back_send.at[w], back_recv.at[w, dy], in_plane(dy, dx)).start()
    for w in waves:
        for dy in (0, 1, 3, 2):
            wait_for(plane_rx.at[w, pl.ds(0, XS if dy else XS - 1), pl.ds(0, pieces[w]), :], back_recv.at[w, dy])
            got = out_ref.at[strip_of(w, lax.rem(y - dy + YS, YS), mine), :]
            remote(got, got, last_send, last_recv, {"sensor": other_core}).start()
    my_half, other_half = out_ref.at[pl.ds(mine, half), :], out_ref.at[pl.ds(theirs, half), :]
    wait_for(other_half, last_recv)
    wait_for(my_half, last_send)
    wait_for(my_half, core_send)
    for w in waves:
        wait_for(plane_rx.at[w, :, pl.ds(0, pieces[w]), :], plane_send.at[w])
        wait_for(z_all.at[w, pl.ds(0, ZS - 1), pl.ds(0, pieces[w]), :], z_send.at[w])
        wait_for(plane_rx.at[w, :, pl.ds(0, pieces[w]), :], back_send.at[w])
    for c in range(CHUNKS):
        all_of(c, a2a_send.at[c])


def normal_matrix(jacobian, residual):
    rows, local = jacobian.shape
    spaces = ZS * XS
    params, cols = rows * spaces, local // spaces
    blocks = params // LANES
    packed = blocks * (blocks + 1) // 2 * LANES
    piece = max(wave_pieces(packed))
    strip = piece * XS
    waves = len(wave_pieces(packed))
    others = YS * XS - 1
    f32, dma = jnp.float32, pltpu.SemaphoreType.DMA
    return pl.pallas_call(
        regroup_kernel,
        out_shape=pltpu.VMEM((packed, LANES), f32),
        in_specs=[pl.BlockSpec(memory_space=pl.ANY), pl.BlockSpec(memory_space=pl.ANY)],
        out_specs=pl.BlockSpec(memory_space=pltpu.VMEM),
        scratch_shapes=[
            pltpu.VMEM((CHUNKS, params, cols // CHUNKS), f32),
            pltpu.VMEM((cols // LANES, LANES), f32),
            pltpu.VMEM((packed, LANES), f32),
            pltpu.VMEM((waves, YS, strip, LANES), f32),
            pltpu.VMEM((waves, others, piece, LANES), f32),
            pltpu.VMEM((waves, ZS, piece, LANES), f32),
            dma((CHUNKS,)), dma,
            dma((CHUNKS,)), dma((CHUNKS,)),
            dma, dma((waves, YS)),
            dma((waves,)), dma((waves,)),
            dma((waves,)), dma((waves,)),
            dma((waves,)), dma((waves, YS)),
            dma, dma,
        ],
        compiler_params=pltpu.CompilerParams(collective_id=0, has_side_effects=True, vmem_limit_bytes=56 << 20),
    )(jacobian, residual.reshape(spaces, -1, LANES))


def solve_kernel(blocks, packed, damping, x_ref, mat):
    wide = blocks + 1
    deep = lax.broadcasted_iota(jnp.int32, (LANES, LANES), 0)
    across = lax.broadcasted_iota(jnp.int32, (LANES, LANES), 1)
    wide_lane = lax.broadcasted_iota(jnp.int32, (1, LANES), 1)
    eye = deep == across
    lam = damping[0]
    scale_rows, scale_cols = [], []
    for b in range(blocks):
        at = block_at(b, b, blocks) * LANES
        diag = jnp.where(eye, packed[at : at + LANES, :], 0.0)
        scale_rows.append(lax.rsqrt(jnp.sum(diag, axis=0, keepdims=True)))
        scale_cols.append(lax.rsqrt(jnp.sum(diag, axis=1, keepdims=True)))
    for b in range(blocks):
        for c in range(b, blocks):
            at = block_at(b, c, blocks) * LANES
            v = packed[at : at + LANES, :]
            if b == c:
                g_row = jnp.where(wide_lane < LANES - 1, v[LANES - 1 :, :], v[LANES - 2 : LANES - 1, 0:1])
                last = jnp.sum(jnp.where(eye, v[:, LANES - 1 :], 0.0), axis=0, keepdims=True)
                v = jnp.where(deep == LANES - 1, last, v)
                v = jnp.where((deep == LANES - 2) & (across == 0), v[0:1, LANES - 2 : LANES - 1], v)
            v = v * scale_cols[b] * scale_rows[c]
            if b == c:
                v = jnp.where(eye, 1.0 + lam, v)
            mat[b * LANES : (b + 1) * LANES, c * LANES : (c + 1) * LANES] = v
            if b == c:
                g_col = jnp.sum(jnp.where(eye, g_row * scale_rows[b], 0.0), axis=1, keepdims=True)
        mat[b * LANES : (b + 1) * LANES, blocks * LANES :] = jnp.broadcast_to(g_col, (LANES, LANES))

    lane = lax.broadcasted_iota(jnp.int32, (8, LANES), 1)
    sub = lax.broadcasted_iota(jnp.int32, (8, LANES), 0)

    def row(v, i):
        return jnp.broadcast_to(v[i : i + 1, :], (8, LANES))

    def invert(t, own):
        wide_by = PANEL // 8
        for h in range(SLAB // PANEL):
            mine = range(h * wide_by, (h + 1) * wide_by)
            first = own + h * PANEL

            def column(v, q):
                return jnp.broadcast_to(v[:, first + q : first + q + 1], (8, LANES))

            cols = [[column(t[i], q) for i in mine] for q in range(PANEL)]
            rows_of = [t[i] for i in mine]
            for p in range(0, PANEL, 2):
                g, k = divmod(p, 8)
                at, bt, ct = row(cols[p][g], k), row(cols[p + 1][g], k), row(cols[p + 1][g], k + 1)
                r = pltpu.reciprocal(at * ct - bt * bt, approx=True)
                if p == 0:
                    tie = r * 0.0
                av, bv, cv = at * r, bt * r, ct * r
                left, right = list(cols[p]), list(cols[p + 1])
                left[g] = left[g] - jnp.where(sub == k, 1.0, 0.0)
                right[g] = right[g] - jnp.where(sub == k + 1, 1.0, 0.0)
                by0 = [x * cv - y * bv for x, y in zip(left, right)]
                by1 = [y * av - x * bv for x, y in zip(left, right)]

                def eliminate(z):
                    z0, z1 = row(z[g], k), row(z[g], k + 1)
                    return [v - (x * z0 + y * z1) for v, x, y in zip(z, by0, by1)]

                for q in range(p + 2, PANEL):
                    cols[q] = eliminate(cols[q])
                rows_of = eliminate(rows_of)
            u_rows = [row(rows_of[q // 8], q % 8) for q in range(PANEL)]
            others = {i: t[i] + tie for i in range(SLAB // 8) if i not in mine}
            parts = {i: [] for i in others}
            for q in range(PANEL):
                for i in others:
                    parts[i].append(column(others[i], q) * u_rows[q])
            new = []
            for i in range(SLAB // 8):
                if i in mine:
                    new.append(rows_of[i - mine[0]])
                    continue
                while len(parts[i]) > 1:
                    parts[i] = [x + y for x, y in zip(parts[i][::2], parts[i][1::2])]
                new.append(t[i] - parts[i][0])
            t = new
        return t

    def slab_step(b, inner):
        top = b * LANES + inner * SLAB
        own = inner * SLAB
        rest = LANES - SLAB - own
        s = mat[top : top + SLAB, b * LANES :]
        t = []
        for i in range(SLAB // 8):
            unit = jnp.where(lane == sub + (rest + 8 * i), 1.0, 0.0)
            t.append(jnp.where((lane >= own) & (lane < own + SLAB), s[8 * i : 8 * i + 8, :LANES], unit))
        inv = jnp.concatenate(invert(t, own), axis=0)
        skip = LANES if inner else 0
        sh, sm, sl = split3(s[:, skip:])
        ih, im, il = split3(inv)
        weights = jnp.concatenate([ih, ih, im, ih, il, im], axis=0)
        stack = jnp.concatenate([sh, sm, sh, sl, sh, sm], axis=0)
        over = (((0,), (0,)), ((), ()))
        u = lax.dot_general(weights, stack, over, preferred_element_type=jnp.float32)[rest : rest + SLAB, :]
        mat[top : top + SLAB, b * LANES + skip :] = u
        count = (blocks - b) * LANES - skip
        if count == 0:
            return

        def later(v):
            v = v[:, :count]
            if inner:
                return v
            edge = jnp.where(lax.broadcasted_iota(jnp.int32, (SLAB, LANES), 1) >= SLAB, v[:, :LANES], jnp.zeros((SLAB, LANES), v.dtype))
            return edge if count == LANES else jnp.concatenate([edge, v[:, LANES:]], axis=1)

        xh, xm, xl = later(sh), later(sm), later(sl)
        uh, um, ul = split3(u)
        left = jnp.concatenate([xh, xh, xm, xh, xl, xm], axis=0)
        right = jnp.concatenate([uh, um, uh, ul, uh, um], axis=0)
        for o in range(0, count, LANES):
            at = b * LANES + skip + o
            prod = lax.dot_general(left[:, o : o + LANES], right[:, o:], over, preferred_element_type=jnp.float32)
            mat[at : at + LANES, at:] -= prod

    for b in range(blocks):
        for inner in range(LANES // SLAB):
            slab_step(b, inner)

    per = LANES // SLAB
    xs = [jnp.zeros((1, LANES), jnp.float32) for _ in range(blocks)]
    for k in reversed(range(blocks * per)):
        b, inner = divmod(k, per)
        u = mat[k * SLAB : (k + 1) * SLAB, :]
        acc = None
        for t in range(b + (inner == per - 1), blocks):
            term = u[:, t * LANES : (t + 1) * LANES] * xs[t]
            acc = term if acc is None else acc + term
        col = u[:, blocks * LANES :]
        if acc is not None:
            col = col - jnp.sum(acc, axis=1, keepdims=True)
        pick = lax.broadcasted_iota(jnp.int32, (SLAB, LANES), 1) == lax.broadcasted_iota(jnp.int32, (SLAB, LANES), 0) + inner * SLAB
        xs[b] = xs[b] + jnp.sum(jnp.where(pick, col, 0.0), axis=0, keepdims=True)
    for b in range(blocks):
        x_ref[b : b + 1, :] = -(xs[b] * scale_rows[b])


def solve(packed, damping, params):
    blocks = params // LANES
    out = pl.pallas_call(
        functools.partial(solve_kernel, blocks),
        out_shape=jax.ShapeDtypeStruct((blocks, LANES), jnp.float32),
        in_specs=[pl.BlockSpec(memory_space=pltpu.VMEM), pl.BlockSpec(memory_space=pltpu.SMEM)],
        out_specs=pl.BlockSpec(memory_space=pltpu.VMEM),
        scratch_shapes=[pltpu.VMEM((params, params + LANES), jnp.float32)],
        compiler_params=pltpu.CompilerParams(vmem_limit_bytes=24 << 20),
    )(packed, damping)
    return out.reshape(params)


def per_device(jacobian, residual, damping):
    params = jacobian.shape[0] * ZS * XS
    return solve(normal_matrix(jacobian, residual), damping, params)


def solution(mesh):
    placed = (P("space", "sensor"), P("sensor"), P())
    return jax.shard_map(per_device, mesh=mesh, in_specs=placed, out_specs=P(), check_vma=False)
```

```python
import functools
import jax
import jax.numpy as jnp
from jax import lax
from jax.experimental import pallas as pl
from jax.experimental.pallas import tpu as pltpu
from jax.sharding import PartitionSpec as P

LANES = 128
MESH = pl.DeviceIdType.MESH
YS, CORES, ZS, XS = 4, 2, 8, 4
CHUNKS = 4
SLAB = 64
PANEL = 16


def split3(v):
    hi = v.astype(jnp.bfloat16)
    rest = v - hi.astype(jnp.float32)
    mid = rest.astype(jnp.bfloat16)
    low = (rest - mid.astype(jnp.float32)).astype(jnp.bfloat16)
    return hi, mid, low


def block_at(b, c, blocks):
    return b * blocks - b * (b - 1) // 2 + (c - b)


def wave_pieces(packed):
    total = packed // (CORES * YS * XS)
    first = total // 16 * 8
    return first, total - first


def regroup_kernel(j_ref, r_ref, out_ref, panel, r_own, pack, core_rx, plane_rx, z_all, own_sem, r_sem,
                   a2a_send, a2a_recv, core_send, core_recv, plane_send, plane_recv, z_send, z_recv,
                   back_send, back_recv, last_send, last_recv):
    sensor, space = lax.axis_index("sensor"), lax.axis_index("space")
    y, core = sensor // CORES, sensor % CORES
    z, x = space // XS, space % XS
    spaces = ZS * XS
    rows = j_ref.shape[0]
    cols = j_ref.shape[1] // spaces
    params = rows * spaces
    blocks = params // LANES
    depth = cols // CHUNKS

    def on_space(dz, dx):
        return lax.rem(z + dz + ZS, ZS) * XS + lax.rem(x + dx + XS, XS)

    def in_plane(dy, dx):
        return {"sensor": lax.rem(y + dy, YS) * CORES + core, "space": on_space(0, dx)}

    other_core = y * CORES + (1 - core)
    my_rows = pl.ds(pl.multiple_of(space * rows, rows), rows)

    def piece_of(device, chunk):
        return j_ref.at[:, pl.ds(pl.multiple_of(device * cols + chunk * depth, depth), depth)]

    own = [pltpu.make_async_copy(piece_of(space, c), panel.at[c, my_rows, :], own_sem.at[c]) for c in range(CHUNKS)]
    for copy in own:
        copy.start()
    r_copy = pltpu.make_async_copy(r_ref.at[space], r_own, r_sem)
    r_copy.start()

    barrier = pltpu.get_barrier_semaphore()

    def greet(d, carry):
        pl.semaphore_signal(barrier, inc=1, device_id={"space": lax.rem(space + d, spaces)}, device_id_type=MESH)
        return carry

    lax.fori_loop(1, spaces, greet, 0)
    pl.semaphore_signal(barrier, inc=1, device_id={"sensor": other_core}, device_id_type=MESH)
    for dy in range(1, YS):
        for dx in range(XS):
            pl.semaphore_signal(barrier, inc=1, device_id=in_plane(dy, dx), device_id_type=MESH)
    pl.semaphore_wait(barrier, spaces - 1 + 1 + (YS - 1) * XS)

    for c in range(CHUNKS):

        def start(d, carry, c=c):
            e = 1 + lax.rem(d + spaces // 2 - 2, spaces - 1)
            to = on_space(e // XS, lax.rem(e, XS))
            pltpu.make_async_remote_copy(
                src_ref=piece_of(to, c),
                dst_ref=panel.at[c, my_rows, :],
                send_sem=a2a_send.at[c],
                recv_sem=a2a_recv.at[c],
                device_id={"space": to},
                device_id_type=MESH,
            ).start()
            return carry

        lax.fori_loop(1, spaces, start, 0)

    def all_of(c, sem):
        others = panel.at[c, pl.ds(0, params - rows), :]
        pltpu.make_async_copy(others, others, sem).wait()

    half = pack.shape[0] // CORES
    pieces = wave_pieces(pack.shape[0])
    waves = range(len(pieces))
    starts = [sum(pieces[:w]) * YS * XS for w in waves]

    def remote(src, dst, send, recv, target):
        return pltpu.make_async_remote_copy(src_ref=src, dst_ref=dst, send_sem=send, recv_sem=recv, device_id=target, device_id_type=MESH)

    mine = pl.multiple_of(core * half, half)
    theirs = pl.multiple_of((1 - core) * half, half)

    def strip_of(w, yy, base):
        strip = pieces[w] * XS
        return pl.ds(pl.multiple_of(base + starts[w] + yy * strip, 8), strip)

    def piece_at(w, yy, xx):
        return pl.ds(pl.multiple_of(mine + starts[w] + (yy * XS + xx) * pieces[w], 8), pieces[w])

    def add_up(parts):
        while len(parts) > 1:
            parts = [u + v for u, v in zip(parts[::2], parts[1::2])]
        return parts[0]

    order = (2, 1, 3, 0)
    core_copies = {}
    for w in waves:
        for dy in order:
            at = strip_of(w, lax.rem(y + dy, YS), theirs)
            core_copies[w, dy] = remote(pack.at[at, :], core_rx.at[w, dy, pl.ds(0, pieces[w] * XS), :], core_send, core_recv.at[w, dy], {"sensor": other_core})

    across = (((1,), (1,)), ((), ()))
    lane = lax.broadcasted_iota(jnp.int32, (1, LANES), 1)
    every = [(b, k) for b in range(blocks) for k in range(b, blocks)]
    share = len(every) // CORES

    def gram_part(part, left, right, first, g_row):
        chosen = every[part * share : (part + 1) * share]
        for b in range(blocks):
            ks = [k for i, k in chosen if i == b]
            if not ks:
                continue
            term = lax.dot_general(
                left[b * LANES : (b + 1) * LANES, :],
                right[ks[0] * LANES : (ks[-1] + 1) * LANES, :],
                across,
                preferred_element_type=jnp.float32,
            )
            for i, k in enumerate(ks):
                at = block_at(b, k, blocks) * LANES
                block = term[:, i * LANES : (i + 1) * LANES]
                pack[at : at + LANES, :] = block if first else pack[at : at + LANES, :] + block
            if g_row is not None and b in ks:
                end = (block_at(b, b, blocks) + 1) * LANES
                g = g_row[:, b * LANES : (b + 1) * LANES]
                pack[end - 1 : end, :] = jnp.where(lane < LANES - 1, g, pack[end - 1 : end, :])
                pack[end - 2 : end - 1, :] = jnp.where(lane == 0, g[:, LANES - 1 :], pack[end - 2 : end - 1, :])

    r_copy.wait()
    for c in range(CHUNKS):
        own[c].wait()
        all_of(c, a2a_recv.at[c])
        hi, mid, low = split3(panel[c])
        left = jnp.concatenate([hi, hi, mid, hi, low, mid], axis=1)
        right = jnp.concatenate([hi, mid, hi, low, hi, mid], axis=1)
        span = depth // LANES
        r_row = jnp.concatenate([r_own[c * span + i : c * span + i + 1, :] for i in range(span)], axis=1)
        rh, rm, rl = split3(jnp.broadcast_to(r_row, (16, depth)))
        r_left = jnp.concatenate([rh, rh, rm, rh, rl, rm], axis=1)
        g = lax.dot_general(r_left, right, across, preferred_element_type=jnp.float32)
        g_row = g[0:1, :] if c == 0 else g_row + g[0:1, :]
        if c < CHUNKS - 1:
            for part in range(CORES):
                gram_part(part, left, right, c == 0, None)
            continue
        for me in range(CORES):

            @pl.when(core == me)
            def _(me=me):
                gram_part(1 - me, left, right, CHUNKS == 1, g_row)
                for copy in core_copies.values():
                    copy.start()
                gram_part(me, left, right, CHUNKS == 1, g_row)

    def wait_for(region, sem):
        pltpu.make_async_copy(region, region, sem).wait()

    offsets = [(dy, dx) for dy in order for dx in order if dy or dx]
    for w in waves:
        for dy in order:
            to_y = lax.rem(y + dy, YS)
            core_copies[w, dy].wait_recv()
            pack[strip_of(w, to_y, mine), :] += core_rx[w, dy, : pieces[w] * XS, :]
            for dx in order:
                if dy or dx:
                    source = pack.at[piece_at(w, to_y, lax.rem(x + dx, XS)), :]
                    landing = plane_rx.at[w, dy * XS + dx - 1, pl.ds(0, pieces[w]), :]
                    remote(source, landing, plane_send.at[w], plane_recv.at[w], in_plane(dy, dx)).start()
    for w in waves:
        wait_for(plane_rx.at[w, :, pl.ds(0, pieces[w]), :], plane_recv.at[w])
        z_all[w, z, : pieces[w], :] = add_up([pack[piece_at(w, y, x), :]] + [plane_rx[w, k, : pieces[w], :] for k in range(YS * XS - 1)])
        for d in (4, 3, 5, 2, 6, 1, 7):
            own_slot = z_all.at[w, z, pl.ds(0, pieces[w]), :]
            remote(own_slot, own_slot, z_send.at[w], z_recv.at[w], {"space": on_space(d, 0)}).start()
    for w in waves:
        wait_for(z_all.at[w, pl.ds(0, ZS - 1), pl.ds(0, pieces[w]), :], z_recv.at[w])
        done = out_ref.at[piece_at(w, y, x), :]
        done[...] = add_up([z_all[w, i, : pieces[w], :] for i in range(ZS)])
        for dy, dx in offsets:
            remote(done, done, back_send.at[w], back_recv.at[w, dy], in_plane(dy, dx)).start()
    for w in waves:
        for dy in (0, 1, 3, 2):
            wait_for(plane_rx.at[w, pl.ds(0, XS if dy else XS - 1), pl.ds(0, pieces[w]), :], back_recv.at[w, dy])
            got = out_ref.at[strip_of(w, lax.rem(y - dy + YS, YS), mine), :]
            remote(got, got, last_send, last_recv, {"sensor": other_core}).start()
    my_half, other_half = out_ref.at[pl.ds(mine, half), :], out_ref.at[pl.ds(theirs, half), :]
    wait_for(other_half, last_recv)
    wait_for(my_half, last_send)
    wait_for(my_half, core_send)
    for w in waves:
        wait_for(plane_rx.at[w, :, pl.ds(0, pieces[w]), :], plane_send.at[w])
        wait_for(z_all.at[w, pl.ds(0, ZS - 1), pl.ds(0, pieces[w]), :], z_send.at[w])
        wait_for(plane_rx.at[w, :, pl.ds(0, pieces[w]), :], back_send.at[w])
    for c in range(CHUNKS):
        all_of(c, a2a_send.at[c])


def normal_matrix(jacobian, residual):
    rows, local = jacobian.shape
    spaces = ZS * XS
    params, cols = rows * spaces, local // spaces
    blocks = params // LANES
    packed = blocks * (blocks + 1) // 2 * LANES
    piece = max(wave_pieces(packed))
    strip = piece * XS
    waves = len(wave_pieces(packed))
    others = YS * XS - 1
    f32, dma = jnp.float32, pltpu.SemaphoreType.DMA
    return pl.pallas_call(
        regroup_kernel,
        out_shape=pltpu.VMEM((packed, LANES), f32),
        in_specs=[pl.BlockSpec(memory_space=pl.ANY), pl.BlockSpec(memory_space=pl.ANY)],
        out_specs=pl.BlockSpec(memory_space=pltpu.VMEM),
        scratch_shapes=[
            pltpu.VMEM((CHUNKS, params, cols // CHUNKS), f32),
            pltpu.VMEM((cols // LANES, LANES), f32),
            pltpu.VMEM((packed, LANES), f32),
            pltpu.VMEM((waves, YS, strip, LANES), f32),
            pltpu.VMEM((waves, others, piece, LANES), f32),
            pltpu.VMEM((waves, ZS, piece, LANES), f32),
            dma((CHUNKS,)), dma,
            dma((CHUNKS,)), dma((CHUNKS,)),
            dma, dma((waves, YS)),
            dma((waves,)), dma((waves,)),
            dma((waves,)), dma((waves,)),
            dma((waves,)), dma((waves, YS)),
            dma, dma,
        ],
        compiler_params=pltpu.CompilerParams(collective_id=0, has_side_effects=True, vmem_limit_bytes=56 << 20),
    )(jacobian, residual.reshape(spaces, -1, LANES))


def solve_kernel(blocks, packed, damping, x_ref, mat):
    wide = blocks + 1
    deep = lax.broadcasted_iota(jnp.int32, (LANES, LANES), 0)
    across = lax.broadcasted_iota(jnp.int32, (LANES, LANES), 1)
    wide_lane = lax.broadcasted_iota(jnp.int32, (1, LANES), 1)
    eye = deep == across
    lam = damping[0]
    scale_rows, scale_cols = [], []
    for b in range(blocks):
        at = block_at(b, b, blocks) * LANES
        diag = jnp.where(eye, packed[at : at + LANES, :], 0.0)
        scale_rows.append(lax.rsqrt(jnp.sum(diag, axis=0, keepdims=True)))
        scale_cols.append(lax.rsqrt(jnp.sum(diag, axis=1, keepdims=True)))
    for b in range(blocks):
        for c in range(b, blocks):
            at = block_at(b, c, blocks) * LANES
            v = packed[at : at + LANES, :]
            if b == c:
                g_row = jnp.where(wide_lane < LANES - 1, v[LANES - 1 :, :], v[LANES - 2 : LANES - 1, 0:1])
                last = jnp.sum(jnp.where(eye, v[:, LANES - 1 :], 0.0), axis=0, keepdims=True)
                v = jnp.where(deep == LANES - 1, last, v)
                v = jnp.where((deep == LANES - 2) & (across == 0), v[0:1, LANES - 2 : LANES - 1], v)
            v = v * scale_cols[b] * scale_rows[c]
            if b == c:
                v = jnp.where(eye, 1.0 + lam, v)
            mat[b * LANES : (b + 1) * LANES, c * LANES : (c + 1) * LANES] = v
            if b == c:
                g_col = jnp.sum(jnp.where(eye, g_row * scale_rows[b], 0.0), axis=1, keepdims=True)
        mat[b * LANES : (b + 1) * LANES, blocks * LANES :] = jnp.broadcast_to(g_col, (LANES, LANES))

    lane = lax.broadcasted_iota(jnp.int32, (8, LANES), 1)
    sub = lax.broadcasted_iota(jnp.int32, (8, LANES), 0)

    def row(v, i):
        return jnp.broadcast_to(v[i : i + 1, :], (8, LANES))

    def invert(t, own):
        wide_by = PANEL // 8
        for h in range(SLAB // PANEL):
            mine = range(h * wide_by, (h + 1) * wide_by)
            first = own + h * PANEL

            def column(v, q):
                return jnp.broadcast_to(v[:, first + q : first + q + 1], (8, LANES))

            cols = [[column(t[i], q) for i in mine] for q in range(PANEL)]
            rows_of = [t[i] for i in mine]
            for p in range(0, PANEL, 2):
                g, k = divmod(p, 8)
                at, bt, ct = row(cols[p][g], k), row(cols[p + 1][g], k), row(cols[p + 1][g], k + 1)
                r = pltpu.reciprocal(at * ct - bt * bt, approx=True)
                if p == 0:
                    tie = r * 0.0
                av, bv, cv = at * r, bt * r, ct * r
                left, right = list(cols[p]), list(cols[p + 1])
                left[g] = left[g] - jnp.where(sub == k, 1.0, 0.0)
                right[g] = right[g] - jnp.where(sub == k + 1, 1.0, 0.0)
                by0 = [x * cv - y * bv for x, y in zip(left, right)]
                by1 = [y * av - x * bv for x, y in zip(left, right)]

                def eliminate(z):
                    z0, z1 = row(z[g], k), row(z[g], k + 1)
                    return [v - (x * z0 + y * z1) for v, x, y in zip(z, by0, by1)]

                for q in range(p + 2, PANEL):
                    cols[q] = eliminate(cols[q])
                rows_of = eliminate(rows_of)
            u_rows = [row(rows_of[q // 8], q % 8) for q in range(PANEL)]
            others = {i: t[i] + tie for i in range(SLAB // 8) if i not in mine}
            parts = {i: [] for i in others}
            for q in range(PANEL):
                for i in others:
                    parts[i].append(column(others[i], q) * u_rows[q])
            new = []
            for i in range(SLAB // 8):
                if i in mine:
                    new.append(rows_of[i - mine[0]])
                    continue
                while len(parts[i]) > 1:
                    parts[i] = [x + y for x, y in zip(parts[i][::2], parts[i][1::2])]
                new.append(t[i] - parts[i][0])
            t = new
        return t

    def slab_step(b, inner):
        top = b * LANES + inner * SLAB
        own = inner * SLAB
        rest = LANES - SLAB - own
        s = mat[top : top + SLAB, b * LANES :]
        t = []
        for i in range(SLAB // 8):
            unit = jnp.where(lane == sub + (rest + 8 * i), 1.0, 0.0)
            t.append(jnp.where((lane >= own) & (lane < own + SLAB), s[8 * i : 8 * i + 8, :LANES], unit))
        inv = jnp.concatenate(invert(t, own), axis=0)
        skip = LANES if inner else 0
        sh, sm, sl = split3(s[:, skip:])
        ih, im, il = split3(inv)
        weights = jnp.concatenate([ih, ih, im, ih, il, im], axis=0)
        stack = jnp.concatenate([sh, sm, sh, sl, sh, sm], axis=0)
        over = (((0,), (0,)), ((), ()))
        u = lax.dot_general(weights, stack, over, preferred_element_type=jnp.float32)[rest : rest + SLAB, :]
        mat[top : top + SLAB, b * LANES + skip :] = u
        count = (blocks - b) * LANES - skip
        if count == 0:
            return

        def later(v):
            v = v[:, :count]
            if inner:
                return v
            edge = jnp.where(lax.broadcasted_iota(jnp.int32, (SLAB, LANES), 1) >= SLAB, v[:, :LANES], jnp.zeros((SLAB, LANES), v.dtype))
            return edge if count == LANES else jnp.concatenate([edge, v[:, LANES:]], axis=1)

        xh, xm, xl = later(sh), later(sm), later(sl)
        uh, um, ul = split3(u)
        left = jnp.concatenate([xh, xh, xm, xh, xl, xm], axis=0)
        right = jnp.concatenate([uh, um, uh, ul, uh, um], axis=0)
        for o in range(0, count, LANES):
            at = b * LANES + skip + o
            prod = lax.dot_general(left[:, o : o + LANES], right[:, o:], over, preferred_element_type=jnp.float32)
            mat[at : at + LANES, at:] -= prod

    for b in range(blocks):
        for inner in range(LANES // SLAB):
            slab_step(b, inner)

    per = LANES // SLAB
    xs = [jnp.zeros((1, LANES), jnp.float32) for _ in range(blocks)]
    for k in reversed(range(blocks * per)):
        b, inner = divmod(k, per)
        u = mat[k * SLAB : (k + 1) * SLAB, :]
        acc = None
        for t in range(b + (inner == per - 1), blocks):
            term = u[:, t * LANES : (t + 1) * LANES] * xs[t]
            acc = term if acc is None else acc + term
        col = u[:, blocks * LANES :]
        if acc is not None:
            col = col - jnp.sum(acc, axis=1, keepdims=True)
        pick = lax.broadcasted_iota(jnp.int32, (SLAB, LANES), 1) == lax.broadcasted_iota(jnp.int32, (SLAB, LANES), 0) + inner * SLAB
        xs[b] = xs[b] + jnp.sum(jnp.where(pick, col, 0.0), axis=0, keepdims=True)
    for b in range(blocks):
        x_ref[b : b + 1, :] = -(xs[b] * scale_rows[b])


def solve(packed, damping, params):
    blocks = params // LANES
    out = pl.pallas_call(
        functools.partial(solve_kernel, blocks),
        out_shape=jax.ShapeDtypeStruct((blocks, LANES), jnp.float32),
        in_specs=[pl.BlockSpec(memory_space=pltpu.VMEM), pl.BlockSpec(memory_space=pltpu.SMEM)],
        out_specs=pl.BlockSpec(memory_space=pltpu.VMEM),
        scratch_shapes=[pltpu.VMEM((params, params + LANES), jnp.float32)],
        compiler_params=pltpu.CompilerParams(vmem_limit_bytes=24 << 20),
    )(packed, damping)
    return out.reshape(params)


def per_device(jacobian, residual, damping):
    params = jacobian.shape[0] * ZS * XS
    return solve(normal_matrix(jacobian, residual), damping, params)


def solution(mesh):
    placed = (P("space", "sensor"), P("sensor"), P())
    return jax.shard_map(per_device, mesh=mesh, in_specs=placed, out_specs=P(), check_vma=False)
```
